256 devices in a mesh: outer: 16 (over z_hi, x, core), tp: 16 (over z_lo, y).
Axes of the slice: x: 4, y: 4, z: 8 (z_hi: 2, z_lo: 4; z = z_hi * 4 + z_lo), core: 2. Of those that a mesh axis runs over, the one named last changes fastest.
Arguments:
- delta: bfloat16 [16, 4096, 4096], P('outer', None, 'tp'), may hold values from -6 to 6
- error: bfloat16 [16, 4096, 4096], P('outer', None, 'tp'), may hold values from -6 to 6
- momentum: bfloat16 [4096, 4096], P(None, 'tp'), may hold values from -3 to 3
- q_init: bfloat16 [4096, 256], P('tp'), may hold values from -6 to 6
Outputs:
- new_error: bfloat16 [16, 4096, 4096], P('outer', None, 'tp')
- new_momentum: bfloat16 [4096, 4096], P(None, 'tp')
- outer_step: bfloat16 [4096, 4096], P(None, 'tp')
- new_factor: bfloat16 [4096, 256], P('tp')
The draws below stay inside these ranges and needn't reach their ends.
All inputs are finite; a program needn't handle non-finite values.
Results may differ from the reference program's by a relative error of at most 0.02.
Values may be sent and summed in bfloat16 or wider, within the bound.
A program may use at most 64 MiB of HBM per device.

```python
import jax
import jax.numpy as jnp
from jax import lax

ROWS = 4096
COLS = 4096
RANK = 256
PODS = 16


def block_levels(stream_key, shape, split, smallest, high):
    factor_of = 1.0
    for dim, shards_of in split:
        draws = jax.random.uniform(jax.random.fold_in(jax.random.fold_in(stream_key, 6), dim), (shards_of,), jnp.float32, smallest / len(split), high / len(split))
        factor_of = factor_of * jnp.repeat(jnp.exp(draws), shape[dim] // shards_of).reshape((-1,) + (1,) * (len(shape) - 1 - dim))
    return factor_of


def centred(key, extent, scale, limit, pieces=(), dtype=jnp.bfloat16):
    drawn = jax.random.normal(key, extent, jnp.float32) * scale
    if len(pieces) > 0:
        drawn = block_levels(key, extent, pieces, -0.22, 0.18) * drawn
    return jnp.clip(drawn, min=-limit, max=limit).astype(dtype)


def setup_inputs(seed: int = 0) -> dict:
    splits = jax.random.split(jax.random.key(seed), 5)
    return {
        "delta": centred(splits[0], (PODS, ROWS, COLS), 1.0, 6.0, ((0, 16), (2, 16))),
        "error": centred(splits[1], (PODS, ROWS, COLS), 0.5, 6.0, ((0, 16), (2, 16))),
        "momentum": centred(splits[2], (ROWS, COLS), 0.2, 3.0, ((1, 16),)),
        "q_init": centred(splits[3], (COLS, RANK), 1.0, 6.0, ((0, 16),)),
    }


def reference(delta, error, momentum, q_init):
    merged = (delta.astype(jnp.float32) + error.astype(jnp.float32)).astype(jnp.bfloat16)

    def add_left(total, slab):
        return (total + jnp.dot(slab.astype(jnp.float32), q_init.astype(jnp.float32), preferred_element_type=jnp.float32), None)
    left, _ = lax.scan(add_left, jnp.zeros((ROWS, RANK), jnp.float32), merged)
    gram = jnp.dot(left.T, left, precision=lax.Precision.HIGHEST)
    lower = jnp.linalg.cholesky(gram)
    basis = lax.linalg.triangular_solve(lower, left, left_side=False, lower=True, transpose_a=True).astype(jnp.bfloat16)

    def add_right(total, slab):
        return (total + jnp.dot(slab.T.astype(jnp.float32), basis.astype(jnp.float32), preferred_element_type=jnp.float32), None)
    right, _ = lax.scan(add_right, jnp.zeros((COLS, RANK), jnp.float32), merged)
    new_factor = (right / PODS).astype(jnp.bfloat16)
    approx = jnp.dot(basis.astype(jnp.float32), new_factor.T.astype(jnp.float32), preferred_element_type=jnp.float32)
    new_error = (merged.astype(jnp.float32) - approx[None]).astype(jnp.bfloat16)
    moment = 0.9 * momentum.astype(jnp.float32) + approx
    outer_step = (0.7 * (approx + 0.9 * moment)).astype(jnp.bfloat16)
    return (new_error, moment.astype(jnp.bfloat16), outer_step, new_factor)
```

```python
import jax
import jax.numpy as jnp
from jax import lax
from jax.experimental import pallas as pl
from jax.experimental.pallas import tpu as pltpu
from jax.sharding import PartitionSpec as P

MESH = pl.DeviceIdType.MESH
F32, BF16 = jnp.float32, jnp.bfloat16
NX, NY, NZ, ZLO = 4, 4, 8, 4
ROWS, RANK, HALF = 4096, 256, 128
MINE = ROWS // 2
PART = MINE // 2
LINE = PART // NX
SUB = LINE // NY
TILE = 16
PODS = 16
OWNERS = 2 * NX
PIECE = RANK // OWNERS


HIGH = lax.Precision.HIGHEST


def mm(a, b, dims):
    return lax.dot_general(a, b, (dims, ((), ())), precision=HIGH, preferred_element_type=F32)


def reciprocal(d):
    guess = pltpu.reciprocal(d, approx=True)
    guess = guess * (2.0 - d * guess)
    return guess * (2.0 - d * guess)


def factor_block(a, between):
    shape = (8, 128)
    lane = lax.broadcasted_iota(jnp.int32, shape, 1)
    row = lax.broadcasted_iota(jnp.int32, shape, 0)
    rest = a
    done = []
    for g in range(16):
        first = 8 * g
        pivots, rest = rest[:8], rest[8:]
        cols = jnp.stack([jnp.broadcast_to(pivots[:, first + c:first + c + 1], shape) for c in range(8)])
        here = (lane >= first) & (lane < first + 8)
        pivots = jnp.where(here, jnp.where(lane - first == row, 1.0, 0.0), pivots)
        upper = jnp.zeros(shape, F32)
        diag = jnp.ones(shape, F32)
        for p in range(0, 8, 2):
            q = p + 1
            at_p, at_q = row == p, row == q
            either = at_p | at_q
            col_p, col_q, cols = cols[0], cols[1], cols[2:]
            d_p = jnp.broadcast_to(col_p[p:p + 1], shape)
            d_pq = jnp.broadcast_to(col_p[q:q + 1], shape)
            d_q = jnp.broadcast_to(col_q[q:q + 1], shape)
            det = d_p * d_q - d_pq * d_pq
            inv = reciprocal(det)
            line_p = jnp.broadcast_to(pivots[p:p + 1], shape)
            line_q = jnp.broadcast_to(pivots[q:q + 1], shape)
            new_p = d_q * line_p - d_pq * line_q
            new_q = d_p * line_q - d_pq * line_p
            over = reciprocal(d_p)
            upper = jnp.where(at_p, pivots, jnp.where(at_q, new_q * over, upper))
            diag = jnp.where(at_p, d_p, jnp.where(at_q, det * over, diag))
            change = jnp.where(at_p, new_p, jnp.where(at_q, new_q, -(col_p * new_p + col_q * new_q)))
            pivots = jnp.where(either, 0.0, pivots) + change * inv
            if p < 6:
                full = cols.shape
                edge_p = jnp.broadcast_to(cols[:, p:p + 1], full)
                edge_q = jnp.broadcast_to(cols[:, q:q + 1], full)
                new_p = d_q[None] * edge_p - d_pq[None] * edge_q
                new_q = d_p[None] * edge_q - d_pq[None] * edge_p
                other = -(col_p[None] * new_p + col_q[None] * new_q)
                change = jnp.where(at_p[None], new_p, jnp.where(at_q[None], new_q, other))
                cols = jnp.where(either[None], 0.0, cols) + change * inv[None]
        done.append(jnp.where(lane <= row + first, upper * (1.0 / jnp.sqrt(diag)), 0.0))
        if g < 15:
            total = jnp.where(here[:1], 0.0, rest)
            for c in range(8):
                total = total - rest[:, first + c:first + c + 1] * pivots[c:c + 1]
            rest = total
        if g in between:
            between[g]()
    return jnp.concatenate(done, axis=0)


def inverse_factor(gram, between):
    on = lax.broadcasted_iota(jnp.int32, gram.shape, 0) == lax.broadcasted_iota(jnp.int32, gram.shape, 1)
    diagonal = jnp.where(on, gram, 0.0)
    scale = 1.0 / jnp.sqrt(jnp.sum(diagonal, axis=0, keepdims=True))
    gram = gram * scale * (1.0 / jnp.sqrt(jnp.sum(diagonal, axis=1, keepdims=True)))
    w11 = factor_block(gram[:128, :128], between[0])
    l21 = mm(gram[128:, :128], w11, ((1,), (1,)))
    w22 = factor_block(gram[128:, 128:] - mm(l21, l21, ((1,), (1,))), between[1])
    w21 = -mm(w22, mm(l21, w11, ((1,), (0,))), ((1,), (0,)))
    top = jnp.concatenate([w11, jnp.zeros((128, 128), F32)], axis=1)
    return jnp.concatenate([top, jnp.concatenate([w21, w22], axis=1)], axis=0) * scale


def device(x, y, z, core):
    return ((z // ZLO) * NX + x) * 2 + core, (z % ZLO) * NY + y


def send(src, dst, send_sem, recv_sem, dev):
    return pltpu.make_async_remote_copy(
        src_ref=src, dst_ref=dst, send_sem=send_sem, recv_sem=recv_sem, device_id=dev, device_id_type=MESH
    )


def exchange(
    delta, error, momentum, q_in, left, merged, held, high, low, new_factor,
    q, dbuf, ebuf, pair_in, pair, s1, keep, r1o, r1d, r1p, o1, s2, r2, s3, r3, o3, g3,
    gpart, gsum, gin, zsum, zsend, zr, zown, zpair, zall,
    ld, cs, cr, p1s, p1r, p2s, p2r, p3s, p3r, a3s, a3r, a2s, a2r, a1s, a1r, axs, axr, acs, acr,
    gs, gr, z1s, z1r, zps, zpr, z2s, z2r,
):
    o, t = lax.axis_index("outer"), lax.axis_index("tp")
    core, x, y = lax.rem(o, 2), lax.rem(o // 2, NX), lax.rem(t, NY)
    z = (o // (2 * NX)) * ZLO + t // NY
    sibling = device(x, y, z, 1 - core)
    c1, c2 = (x, y), (y, x)

    def peer1(h, v):
        return device(v, y, z, core) if h == 0 else device(x, v, z, core)

    def peer2(h, v):
        return device(x, v, z, core) if h == 0 else device(v, y, z, core)

    def turn(v, i, n):
        return lax.rem(v + i, n)

    def rows(start, size):
        return pl.ds(pl.multiple_of(start, TILE), size)

    mine, theirs = core * MINE, (1 - core) * MINE

    def line(h, i):
        return h * PART + turn(c1[h], i, NX) * LINE

    order = [(i, h) for i in (2, 1, 3, 0) for h in range(2)]

    def loads(k, base, i, h):
        src = rows(base + line(h, i), LINE)
        return (
            pltpu.make_async_copy(delta.at[0, src], dbuf.at[src], ld.at[k, 0]),
            pltpu.make_async_copy(error.at[0, src], ebuf.at[src], ld.at[k, 1]),
        )

    barrier = pltpu.get_barrier_semaphore()
    greeted = [sibling]
    greeted += [device(turn(x, i, NX), y, z, core) for i in range(1, NX)]
    greeted += [device(x, turn(y, i, NY), z, core) for i in range(1, NY)]
    greeted += [device(x, y, turn(z, i, NZ), core) for i in range(1, NZ)]
    greeted += [device(turn(x, i, NX), y, z, 1 - core) for i in range(1, NX)]
    for dev in greeted:
        pl.semaphore_signal(barrier, inc=1, device_id=dev, device_id_type=MESH)

    steps = [loads(k, theirs, i, h) for k, (i, h) in enumerate(order)]
    steps += [loads(8 + k, mine, i, h) for k, (i, h) in enumerate(order)]
    for step in steps:
        for copy in step:
            copy.start()
    load_q = pltpu.make_async_copy(q_in, q, ld.at[16, 0])
    load_q.start()

    pending = []

    def go(*args):
        copy = send(*args)
        copy.start()
        pending.append(copy)

    def merge(k, base, i, h):
        for copy in steps[k]:
            copy.wait()
        block = rows(base + line(h, i), LINE)
        total = (dbuf[block, :].astype(F32) + ebuf[block, :].astype(F32)).astype(BF16)
        merged[block, :] = total
        return block, total

    for k, (i, h) in enumerate(order):
        block, _ = merge(k, theirs, i, h)
        if k == 0:
            pl.semaphore_wait(barrier, len(greeted))
        here = rows(line(h, i), LINE)
        go(merged.at[block], pair_in.at[here], cs.at[h, i], cr.at[h, i], sibling)
    load_q.wait()

    half = LINE // 2

    def up(h):
        return peer1(h, turn(c1[h], 1, NX))

    def down(h):
        return peer1(h, turn(c1[h], NX - 1, NX))

    for k, (i, h) in enumerate(order):
        _, total = merge(8 + k, mine, i, h)
        at = line(h, i)
        here = rows(at, LINE)
        send(pair_in.at[here], pair_in.at[here], cs.at[h, i], cr.at[h, i], sibling).wait_recv()
        both = (total.astype(F32) + pair_in[here, :].astype(F32)).astype(BF16)
        pair[here, :] = both
        term = jnp.dot(both, q[...], preferred_element_type=F32)
        first, second = rows(at, half), rows(at + half, half)
        if i == 2:
            s1[here, :] = term.astype(BF16)
            go(s1.at[first], r1d.at[h, 0], p1s.at[h, 0, 0], p1r.at[h, 0, 0], up(h))
            go(s1.at[second], r1d.at[h, 1], p1s.at[h, 1, 0], p1r.at[h, 1, 0], down(h))
        elif i == 1:
            s1[second, :] = term[half:].astype(BF16)
            go(s1.at[second], r1o.at[h, 0], p1s.at[h, 0, 1], p1r.at[h, 0, 1], up(h))
            keep[h, 0] = term[:half]
        elif i == 3:
            s1[first, :] = term[:half].astype(BF16)
            go(s1.at[first], r1o.at[h, 1], p1s.at[h, 1, 1], p1r.at[h, 1, 1], down(h))
            keep[h, 1] = term[half:]
        else:
            o1[h] = term
    for h in range(2):
        send(r1d.at[h, 0], r1d.at[h, 0], p1s.at[h, 0, 0], p1r.at[h, 0, 0], down(h)).wait_recv()
        first = rows(line(h, 1), half)
        s1[first, :] = (keep[h, 0] + r1d[h, 0].astype(F32)).astype(BF16)
        go(s1.at[first], r1p.at[h, 0], p1s.at[h, 0, 2], p1r.at[h, 0, 2], up(h))
        send(r1d.at[h, 1], r1d.at[h, 1], p1s.at[h, 1, 0], p1r.at[h, 1, 0], up(h)).wait_recv()
        second = rows(line(h, 3) + half, half)
        s1[second, :] = (keep[h, 1] + r1d[h, 1].astype(F32)).astype(BF16)
        go(s1.at[second], r1p.at[h, 1], p1s.at[h, 1, 2], p1r.at[h, 1, 2], down(h))

    load_momentum = pltpu.make_async_copy(momentum, held, ld.at[16, 1])
    load_momentum.start()

    for h in range(2):
        send(r1o.at[h, 0], r1o.at[h, 0], p1s.at[h, 0, 1], p1r.at[h, 0, 1], down(h)).wait_recv()
        send(r1o.at[h, 1], r1o.at[h, 1], p1s.at[h, 1, 1], p1r.at[h, 1, 1], up(h)).wait_recv()
        send(r1p.at[h, 0], r1p.at[h, 0], p1s.at[h, 0, 2], p1r.at[h, 0, 2], down(h)).wait_recv()
        send(r1p.at[h, 1], r1p.at[h, 1], p1s.at[h, 1, 2], p1r.at[h, 1, 2], up(h)).wait_recv()
        o1[h, :half] += r1p[h, 0].astype(F32) + r1o[h, 1].astype(F32)
        o1[h, half:] += r1o[h, 0].astype(F32) + r1p[h, 1].astype(F32)
        s2[h] = o1[h].astype(BF16)
        for i in (2, 1, 3):
            b = turn(c2[h], i, NY)
            go(s2.at[h, rows(b * SUB, SUB)], r2.at[h, c2[h]], p2s.at[h, b], p2r.at[h, c2[h]], peer2(h, b))
    for h in range(2):
        for i in range(1, NY):
            b = turn(c2[h], i, NY)
            send(r2.at[h, b], r2.at[h, b], p2s.at[h, b], p2r.at[h, b], peer2(h, b)).wait_recv()
        total = o1[h, rows(c2[h] * SUB, SUB), :]
        for i in range(1, NY):
            total += r2[h, turn(c2[h], i, NY)].astype(F32)
        for c in range(2):
            o3[h, c] = total[:, c * HALF:(c + 1) * HALF]
            s3[h, c] = total[:, c * HALF:(c + 1) * HALF].astype(BF16)

    far = (4, 3, 5, 2, 6, 1, 7)

    def spot(v):
        return v // 4, rows((v % 4) * TILE, TILE)

    for i in far:
        b = turn(z, i, NZ)
        c, at = spot(b)
        go(s3.at[:, c, at], r3.at[z], p3s.at[b], p3r.at[z], device(x, y, b, core))
    for i in far:
        b = turn(z, i, NZ)
        send(r3.at[b], r3.at[b], p3s.at[b], p3r.at[b], device(x, y, b, core)).wait_recv()

    def sub(h, i, j):
        return rows(mine + line(h, i) + turn(c2[h], j, NY) * SUB, SUB)

    c, at = spot(z)
    for h in range(2):
        total = o3[h, c, at, :]
        for i in range(1, NZ):
            total += r3[turn(z, i, NZ), h].astype(F32)
        g3[z, h] = total.astype(BF16)
    for i in far:
        b = turn(z, i, NZ)
        go(g3.at[z], g3.at[z], a3s.at[b], a3r.at[z], device(x, y, b, core))

    def along(h, j):
        at, b = left.at[sub(h, 0, j)], turn(c2[h], j, NY)
        go(at, at, a1s.at[h, 0, b], a1r.at[h, 0, b], up(h))
        go(at, at, a1s.at[h, 1, b], a1r.at[h, 1, b], down(h))

    def arrive(h, side, j):
        at, b = left.at[sub(h, 3 if side == 0 else 1, j)], turn(c2[h], j, NY)
        send(at, at, a1s.at[h, side, b], a1r.at[h, side, b], down(h) if side == 0 else up(h)).wait_recv()

    def relay(h, side, j):
        at, b = left.at[sub(h, 3 if side == 0 else 1, j)], turn(c2[h], j, NY)
        go(at, at, axs.at[h, b], axr.at[h, b], up(h) if side == 0 else down(h))

    def cross(h, i):
        at = left.at[rows(mine + line(h, i), LINE)]
        go(at, at, acs.at[h, i], acr.at[h, i], sibling)

    zsum[...] = jnp.zeros_like(zsum)

    def products(h, i):
        within = line(h, i)
        part = left[rows(mine + within, LINE), :]
        both = jnp.concatenate([part, pair[rows(within, LINE), :]], axis=1)
        product = lax.dot_general(part, both, (((0,), (0,)), ((), ())), preferred_element_type=F32)
        gpart[h * NX + turn(c1[h], i, NX)] = product[:, :RANK]
        zsum[...] += product[:, RANK:]

    for i in far:
        b = turn(z, i, NZ)
        send(g3.at[b], g3.at[b], a3s.at[b], a3r.at[b], device(x, y, b, core)).wait_recv()
    for h in range(2):
        left[sub(h, 0, 0), :] = jnp.concatenate(
            [jnp.concatenate([g3[c * 4 + v, h] for c in range(2)], axis=1) for v in range(4)], axis=0
        )
        at = left.at[sub(h, 0, 0)]
        for i in (2, 1, 3):
            b = turn(c2[h], i, NY)
            go(at, at, a2s.at[h, b], a2r.at[h, c2[h]], peer2(h, b))
        along(h, 0)
    for j in (1, 3, 2):
        for h in range(2):
            at, b = left.at[sub(h, 0, j)], turn(c2[h], j, NY)
            send(at, at, a2s.at[h, b], a2r.at[h, b], peer2(h, b)).wait_recv()
            along(h, j)
    for h in range(2):
        arrive(h, 0, 0)
        relay(h, 0, 0)
    products(0, 0)
    for j, side in ((1, 0), (3, 1)):
        for h in range(2):
            arrive(h, side, j)
            relay(h, side, j)
    products(1, 0)
    for h in range(2):
        arrive(h, 1, 2)
        relay(h, 1, 2)
        cross(h, 0)
    for h in range(2):
        arrive(h, 0, 3)
        arrive(h, 0, 2)
        cross(h, 3)
        products(h, 3)
    for h in range(2):
        arrive(h, 1, 0)
        arrive(h, 1, 1)
        cross(h, 1)
        products(h, 1)
    for h in range(2):
        for j in (0, 1, 3, 2):
            at, b = left.at[sub(h, 2, j)], turn(c2[h], j, NY)
            dev = down(h) if j < 2 else up(h)
            send(at, at, axs.at[h, b], axr.at[h, b], dev).wait_recv()
        products(h, 2)

    total = gpart[0]
    for i in range(1, 2 * NX):
        total += gpart[i]
    gsum[...] = total
    go(gsum, gin, gs.at[0], gr.at[0], sibling)

    owner = x * 2 + core
    others = [(turn(x, i, NX), lax.rem(core + e, 2)) for i in range(NX) for e in range(2) if i or e]

    def piece(v, c):
        return rows((v * 2 + c) * PIECE, PIECE)

    zsend[...] = zsum[...].astype(BF16)
    for v, c in others:
        go(zsend.at[piece(v, c)], zr.at[owner], z1s.at[v * 2 + c], z1r.at[owner], device(v, y, z, c))
    for h in range(2):
        cross(h, 2)
    across = device(x, y, turn(z, ZLO, NZ), core)

    def add_pieces():
        for v, c in others:
            e = v * 2 + c
            send(zr.at[e], zr.at[e], z1s.at[e], z1r.at[e], device(v, y, z, c)).wait_recv()
        total = zsum[piece(x, core), :]
        for v, c in others:
            total += zr[v * 2 + c].astype(F32)
        zown[...] = total.astype(BF16)
        go(zown, zpair, zps.at[0], zpr.at[0], across)

    def add_across():
        send(zpair, zpair, zps.at[0], zpr.at[0], across).wait_recv()
        here = piece(x, core)
        zall[here, :] = (zown[...].astype(F32) + zpair[...].astype(F32)).astype(BF16)
        for v, c in others:
            go(zall.at[here], zall.at[here], z2s.at[v * 2 + c], z2r.at[owner], device(v, y, z, c))

    send(gin, gin, gs.at[0], gr.at[0], sibling).wait_recv()
    inverse = inverse_factor(gsum[...] + gin[...], ({12: add_pieces}, {8: add_across}))
    for v, c in others:
        e = v * 2 + c
        send(zall.at[piece(v, c)], zall.at[piece(v, c)], z2s.at[e], z2r.at[e], device(v, y, z, c)).wait_recv()
    factor = (mm(inverse, zall[...].astype(F32), ((1,), (0,))) / PODS).astype(BF16)
    new_factor[...] = factor.T
    mix = mm(inverse, factor.astype(F32), ((0,), (0,)))
    head = mix.astype(BF16)
    high[...] = head
    low[...] = (mix - head.astype(F32)).astype(BF16)

    for h in range(2):
        for i in range(NX):
            at = left.at[rows(theirs + line(h, i), LINE)]
            send(at, at, acs.at[h, i], acr.at[h, i], sibling).wait_recv()
    load_momentum.wait()
    for copy in pending:
        copy.wait_send()


def gather(delta, error, momentum, q):
    vmem, hbm = (pl.BlockSpec(memory_space=s) for s in (pltpu.VMEM, pltpu.HBM))
    dma = pltpu.SemaphoreType.DMA
    wide, square = (ROWS, RANK), (RANK, RANK)
    return pl.pallas_call(
        exchange,
        out_shape=(
            jax.ShapeDtypeStruct(wide, BF16),
            jax.ShapeDtypeStruct(wide, BF16),
            jax.ShapeDtypeStruct(wide, BF16),
            jax.ShapeDtypeStruct(square, BF16),
            jax.ShapeDtypeStruct(square, BF16),
            jax.ShapeDtypeStruct(square, BF16),
        ),
        in_specs=[hbm] * 4,
        out_specs=(vmem,) * 6,
        scratch_shapes=[
            pltpu.VMEM(square, BF16),
            pltpu.VMEM(wide, BF16),
            pltpu.VMEM(wide, BF16),
            pltpu.VMEM((MINE, RANK), BF16),
            pltpu.VMEM((MINE, RANK), BF16),
            pltpu.VMEM((MINE, RANK), BF16),
            pltpu.VMEM((2, 2, LINE // 2, RANK), F32),
            pltpu.VMEM((2, 2, LINE // 2, RANK), BF16),
            pltpu.VMEM((2, 2, LINE // 2, RANK), BF16),
            pltpu.VMEM((2, 2, LINE // 2, RANK), BF16),
            pltpu.VMEM((2, LINE, RANK), F32),
            pltpu.VMEM((2, LINE, RANK), BF16),
            pltpu.VMEM((2, NY, SUB, RANK), BF16),
            pltpu.VMEM((2, 2, SUB, HALF), BF16),
            pltpu.VMEM((NZ, 2, TILE, HALF), BF16),
            pltpu.VMEM((2, 2, SUB, HALF), F32),
            pltpu.VMEM((NZ, 2, TILE, HALF), BF16),
            pltpu.VMEM((2 * NX,) + square, F32),
            pltpu.VMEM(square, F32),
            pltpu.VMEM(square, F32),
            pltpu.VMEM(square, F32),
            pltpu.VMEM(square, BF16),
            pltpu.VMEM((OWNERS, PIECE, RANK), BF16),
            pltpu.VMEM((PIECE, RANK), BF16),
            pltpu.VMEM((PIECE, RANK), BF16),
            pltpu.VMEM(square, BF16),
            dma((17, 2)),
            dma((2, NX)), dma((2, NX)),
            dma((2, 2, 3)), dma((2, 2, 3)),
            dma((2, NY)), dma((2, NY)),
            dma((NZ,)), dma((NZ,)),
            dma((NZ,)), dma((NZ,)),
            dma((2, NY)), dma((2, NY)),
            dma((2, 2, NY)), dma((2, 2, NY)),
            dma((2, NY)), dma((2, NY)),
            dma((2, NX)), dma((2, NX)),
            dma((1,)), dma((1,)),
            dma((OWNERS,)), dma((OWNERS,)),
            dma((1,)), dma((1,)),
            dma((OWNERS,)), dma((OWNERS,)),
        ],
        compiler_params=pltpu.CompilerParams(collective_id=0, has_side_effects=True, vmem_limit_bytes=32 << 20),
        cost_estimate=pl.CostEstimate(flops=6 * ROWS * RANK * RANK, bytes_accessed=5 * ROWS * RANK * 2, transcendentals=0),
        name="gather_left",
    )(*(pltpu.with_memory_space_constraint(a, pltpu.HBM) for a in (delta, error, momentum, q)))


def finish(left, merged, momentum, high, low, factor, new_error, new_momentum, outer_step, new_factor, e, m, s, sem):
    size, count = ROWS // 8, 8
    copies = [pltpu.make_async_copy(factor, new_factor, sem.at[count, 0])]
    copies[0].start()
    for i in range(count):
        at = pl.ds(i * size, size)
        block = left[at, :]
        approx = jnp.dot(block, high[...], preferred_element_type=F32) + jnp.dot(
            block, low[...], preferred_element_type=F32
        )
        e[at, :] = (merged[at, :].astype(F32) - approx).astype(BF16)
        moment = 0.9 * momentum[at, :].astype(F32) + approx
        m[at, :] = moment.astype(BF16)
        s[at, :] = (0.7 * (approx + 0.9 * moment)).astype(BF16)
        for k, (src, dst) in enumerate(((e, new_error.at[0, at]), (m, new_momentum.at[at]), (s, outer_step.at[at]))):
            copies.append(pltpu.make_async_copy(src.at[at], dst, sem.at[i, k]))
            copies[-1].start()
    for copy in copies:
        copy.wait()


def outputs(left, merged, momentum, high, low, factor):
    any_, vmem = pl.BlockSpec(memory_space=pl.ANY), pl.BlockSpec(memory_space=pltpu.VMEM)
    wide = (ROWS, RANK)
    return pl.pallas_call(
        finish,
        out_shape=(
            jax.ShapeDtypeStruct((1,) + wide, BF16),
            jax.ShapeDtypeStruct(wide, BF16),
            jax.ShapeDtypeStruct(wide, BF16),
            jax.ShapeDtypeStruct((RANK, RANK), BF16),
        ),
        in_specs=[vmem] * 6,
        out_specs=(any_,) * 4,
        scratch_shapes=[pltpu.VMEM(wide, BF16)] * 3 + [pltpu.SemaphoreType.DMA((9, 3))],
        compiler_params=pltpu.CompilerParams(vmem_limit_bytes=24 << 20),
        cost_estimate=pl.CostEstimate(flops=4 * ROWS * RANK * RANK, bytes_accessed=6 * ROWS * RANK * 2, transcendentals=0),
        name="outputs",
    )(left, merged, momentum, high, low, factor)


def body(delta, error, momentum, q_init):
    left, merged, held, high, low, factor = gather(delta, error, momentum, q_init)
    return outputs(left, merged, held, high, low, factor)


def solution(mesh):
    placed = (P("outer", None, "tp"), P("outer", None, "tp"), P(None, "tp"), P("tp", None))
    return jax.shard_map(
        body,
        mesh=mesh,
        in_specs=placed,
        out_specs=(P("outer", None, "tp"), P(None, "tp"), P(None, "tp"), P("tp", None)),
        check_vma=False,
    )
```

```python
import jax
import jax.numpy as jnp
from jax import lax
from jax.experimental import pallas as pl
from jax.experimental.pallas import tpu as pltpu
from jax.sharding import PartitionSpec as P

MESH = pl.DeviceIdType.MESH
F32, BF16 = jnp.float32, jnp.bfloat16
NX, NY, NZ, ZLO = 4, 4, 8, 4
ROWS, RANK, HALF = 4096, 256, 128
MINE = ROWS // 2
PART = MINE // 2
LINE = PART // NX
SUB = LINE // NY
TILE = 16
PODS = 16
OWNERS = 2 * NX
PIECE = RANK // OWNERS


HIGH = lax.Precision.HIGHEST


def mm(a, b, dims):
    return lax.dot_general(a, b, (dims, ((), ())), precision=HIGH, preferred_element_type=F32)


def reciprocal(d):
    return pltpu.reciprocal(d, approx=True)


def factor_block(a, between):
    tile = (8, 128)
    lane = lax.broadcasted_iota(jnp.int32, tile, 1)
    row = lax.broadcasted_iota(jnp.int32, tile, 0)
    tiles = a.reshape(16, 8, 128)
    both, rest = tiles[:2], tiles[2:]
    done = []
    for g in range(16):
        first = 8 * g
        shape = both.shape
        below = shape[0] - 1
        cols = [jnp.broadcast_to(both[:, :, first + c:first + c + 1], shape) for c in range(8)]
        here = (lane >= first) & (lane < first + 8)
        start = [jnp.where(here, jnp.where(lane - first == row, 1.0, 0.0), both[0])]
        start += [jnp.where(here, 0.0, both[1])] * below
        both = jnp.stack(start)
        diag = jnp.ones(tile, F32)

        def spread(x, r):
            return jnp.broadcast_to(x[0, r:r + 1], tile)

        def after(r, x):
            top = jnp.where(row > r, x[:1], 0.0)
            return jnp.concatenate([top, x[1:]], axis=0) if below else top

        for p in range(0, 8, 2):
            q = p + 1
            d_p, d_pq, d_q = spread(cols[p], p), spread(cols[p], q), spread(cols[q], q)
            det = d_p * d_q - d_pq * d_pq
            inv_p = reciprocal(d_p)
            inv_q = d_p * reciprocal(det)
            ratio = d_pq * inv_p
            line_p = spread(both, p)
            line_q = spread(both, q) - ratio * line_p
            diag = jnp.where(row == p, d_p, jnp.where(row == q, det * inv_p, diag))
            part_p = after(p, cols[p] * inv_p)
            part_q = after(q, (cols[q] - part_p * d_pq) * inv_q)
            both = both - part_p * line_p - part_q * line_q
            for k in range(q + 1, 8):
                edge_p = spread(cols[k], p)
                edge_q = spread(cols[k], q) - ratio * edge_p
                cols[k] = cols[k] - part_p * edge_p - part_q * edge_q
        upper = both[0]
        done.append(jnp.where(lane <= row + first, upper * (1.0 / jnp.sqrt(diag)), 0.0))
        if g < 14:
            factors = (upper / diag).T[first + 16:].reshape(rest.shape[0], 8, 8)
            rest = jnp.where(here, 0.0, rest)
            for c in range(8):
                rest = rest - factors[:, :, c:c + 1] * upper[c:c + 1]
            both = jnp.concatenate([both[1:], rest[:1]], axis=0)
            rest = rest[1:] if g < 13 else None
        elif g < 15:
            both = both[1:]
        if g in between:
            between[g]()
    return jnp.concatenate(done, axis=0)


def inverse_factor(gram, between):
    on = lax.broadcasted_iota(jnp.int32, gram.shape, 0) == lax.broadcasted_iota(jnp.int32, gram.shape, 1)
    diagonal = jnp.where(on, gram, 0.0)
    scale = 1.0 / jnp.sqrt(jnp.sum(diagonal, axis=0, keepdims=True))
    gram = gram * scale * (1.0 / jnp.sqrt(jnp.sum(diagonal, axis=1, keepdims=True)))
    w11 = factor_block(gram[:128, :128], between[0])
    l21 = mm(gram[128:, :128], w11, ((1,), (1,)))
    w22 = factor_block(gram[128:, 128:] - mm(l21, l21, ((1,), (1,))), between[1])
    w21 = -mm(w22, mm(l21, w11, ((1,), (0,))), ((1,), (0,)))
    top = jnp.concatenate([w11, jnp.zeros((128, 128), F32)], axis=1)
    return jnp.concatenate([top, jnp.concatenate([w21, w22], axis=1)], axis=0) * scale


def device(x, y, z, core):
    return ((z // ZLO) * NX + x) * 2 + core, (z % ZLO) * NY + y


def send(src, dst, send_sem, recv_sem, dev):
    return pltpu.make_async_remote_copy(
        src_ref=src, dst_ref=dst, send_sem=send_sem, recv_sem=recv_sem, device_id=dev, device_id_type=MESH
    )


def exchange(
    delta, error, momentum, q_in, left, merged, held, high, low, new_factor,
    q, dbuf, ebuf, pair_in, s1, xs, rx, sx, keep, r1o, r1d, r1p, o1, s2, r2, s3, r3, o3, g3,
    gpart, gsum, gin, zsum, zsend, zr, zown, zpair, zall,
    ld, ss, cr, p1d, p1r, p2r, oner, a2r, a1r, axr,
):
    o, t = lax.axis_index("outer"), lax.axis_index("tp")
    core, x, y = lax.rem(o, 2), lax.rem(o // 2, NX), lax.rem(t, NY)
    z = (o // (2 * NX)) * ZLO + t // NY
    sibling = device(x, y, z, 1 - core)
    c1, c2 = (x, y), (y, x)

    def peer1(h, v):
        return device(v, y, z, core) if h == 0 else device(x, v, z, core)

    def peer2(h, v):
        return device(x, v, z, core) if h == 0 else device(v, y, z, core)

    def turn(v, i, n):
        return lax.rem(v + i, n)

    def rows(start, size):
        return pl.ds(pl.multiple_of(start, TILE), size)

    mine, theirs = core * MINE, (1 - core) * MINE

    def line(h, i):
        return h * PART + turn(c1[h], i, NX) * LINE

    order = [(whose, i) for whose in range(2) for i in (2, 1, 3, 0)]

    def loads(whose, i, h):
        src, k = rows((mine if whose else theirs) + line(h, i), LINE), whose * NX + i
        return (
            pltpu.make_async_copy(delta.at[0, src], dbuf.at[src], ld.at[k]),
            pltpu.make_async_copy(error.at[0, src], ebuf.at[src], ld.at[k]),
        )

    barrier = pltpu.get_barrier_semaphore()
    greeted = [sibling]
    greeted += [device(turn(x, i, NX), y, z, core) for i in range(1, NX)]
    greeted += [device(x, turn(y, i, NY), z, core) for i in range(1, NY)]
    greeted += [device(x, y, turn(z, i, NZ), core) for i in range(1, NZ)]
    greeted += [device(turn(x, i, NX), y, z, 1 - core) for i in range(1, NX)]
    for dev in greeted:
        pl.semaphore_signal(barrier, inc=1, device_id=dev, device_id_type=MESH)

    for whose, i in order:
        for h in range(2):
            for copy in loads(whose, i, h):
                copy.start()
    load_q = pltpu.make_async_copy(q_in, q, ld.at[8])
    load_q.start()

    stages = ("core", "first", "second", "z", "merged", "tiles", "gather", "lines", "cross", "gram", "right", "across", "back")

    def go(stage, src, dst, recv_sem, dev):
        send(src, dst, ss.at[stages.index(stage)], recv_sem, dev).start()

    def sent(stage, ref):
        sem = ss.at[stages.index(stage)]
        send(ref, ref, sem, sem, sibling).wait_send()

    def landed(ref, sem):
        send(ref, ref, ss.at[0], sem, sibling).wait_recv()

    def span(ref, size):
        return ref.at[pl.ds(0, size)]

    def merge(whose, i, h):
        if h == 0:
            every = span(dbuf, 4 * LINE)
            pltpu.make_async_copy(every, every, ld.at[whose * NX + i]).wait()
        block = rows((mine if whose else theirs) + line(h, i), LINE)
        total = (dbuf[block, :].astype(F32) + ebuf[block, :].astype(F32)).astype(BF16)
        merged[block, :] = total
        return block, total.astype(F32)

    half = LINE // 2

    def up(h):
        return peer1(h, turn(c1[h], 1, NX))

    def down(h):
        return peer1(h, turn(c1[h], NX - 1, NX))

    def give(i, h):
        block, _ = merge(0, i, h)
        here = rows(line(h, i), LINE)
        go("core", merged.at[block], pair_in.at[here], cr.at[i], sibling)

    def take(i, h):
        _, total = merge(1, i, h)
        at = line(h, i)
        here = rows(at, LINE)
        if h == 0:
            landed(span(pair_in, 2 * LINE), cr.at[i])
        total = total + pair_in[here, :].astype(F32)
        if h == 1:
            both = total.astype(BF16)
            xs[turn(y, i, NY)] = both.reshape(NX, SUB, RANK)
            total = jnp.dot(both, q[...], preferred_element_type=F32)
        first, second = rows(at, half), rows(at + half, half)
        if i == 2:
            s1[here, :] = total.astype(BF16)
            go("first", s1.at[first], r1d.at[h, 0], p1d.at[h, 0], up(h))
            go("first", s1.at[second], r1d.at[h, 1], p1d.at[h, 1], down(h))
        elif i == 1:
            s1[second, :] = total[half:].astype(BF16)
            go("first", s1.at[second], r1o.at[h, 0], p1r.at[h], up(h))
            keep[h, 0] = total[:half]
        elif i == 3:
            s1[first, :] = total[:half].astype(BF16)
            go("first", s1.at[first], r1o.at[h, 1], p1r.at[h], down(h))
            keep[h, 1] = total[half:]
        else:
            o1[h] = total

    for n, (whose, i) in enumerate(order):
        if n == 0:
            pl.semaphore_wait(barrier, len(greeted))
        if n == 2:
            load_q.wait()
        if n == 7:
            for h in range(2):
                landed(r1d.at[h, 0], p1d.at[h, 0])
                first = rows(line(h, 1), half)
                s1[first, :] = (keep[h, 0] + r1d[h, 0].astype(F32)).astype(BF16)
                go("first", s1.at[first], r1p.at[h, 0], p1r.at[h], up(h))
                landed(r1d.at[h, 1], p1d.at[h, 1])
                second = rows(line(h, 3) + half, half)
                s1[second, :] = (keep[h, 1] + r1d[h, 1].astype(F32)).astype(BF16)
                go("first", s1.at[second], r1p.at[h, 1], p1r.at[h], down(h))
        for h in range(2):
            if whose:
                take(i, h)
            else:
                give(i, h)

    load_momentum = pltpu.make_async_copy(momentum, held, ld.at[9])
    load_momentum.start()

    for h in range(2):
        landed(span(s1, 2 * LINE), p1r.at[h])
        o1[h, :half] += r1p[h, 0].astype(F32) + r1o[h, 1].astype(F32)
        o1[h, half:] += r1o[h, 0].astype(F32) + r1p[h, 1].astype(F32)
        if h == 0:
            sx[0] = o1[0].astype(BF16)
            o1[0] = jnp.dot(sx[0], q[...], preferred_element_type=F32)
        s2[h] = o1[h].astype(BF16)
        for i in (2, 1, 3):
            b = turn(c2[h], i, NY)
            go("second", s2.at[h, rows(b * SUB, SUB)], r2.at[h, c2[h]], p2r.at[h], peer2(h, b))
    for h in range(2):
        landed(r2.at[h, pl.ds(0, NY - 1)], p2r.at[h])
        total = o1[h, rows(c2[h] * SUB, SUB), :]
        for i in range(1, NY):
            total += r2[h, turn(c2[h], i, NY)].astype(F32)
        for c in range(2):
            o3[h, c] = total[:, c * HALF:(c + 1) * HALF]
            s3[h, c] = total[:, c * HALF:(c + 1) * HALF].astype(BF16)

    far = (4, 3, 5, 2, 6, 1, 7)

    def spot(v):
        return v // 4, rows((v % 4) * TILE, TILE)

    for i in far:
        b = turn(z, i, NZ)
        c, at = spot(b)
        go("z", s3.at[:, c, at], r3.at[z], oner.at[0], device(x, y, b, core))
    for i in (2, 1, 3):
        b = turn(x, i, NX)
        go("merged", xs.at[:, b], rx.at[x], oner.at[1], device(b, y, z, core))
    sent("core", span(left, 2 * PART))
    sent("first", span(left, 6 * LINE))
    sent("second", span(left, 6 * SUB))
    landed(span(r3, NZ - 1), oner.at[0])

    def sub(h, i, j):
        return rows(mine + line(h, i) + turn(c2[h], j, NY) * SUB, SUB)

    c, at = spot(z)
    for h in range(2):
        total = o3[h, c, at, :]
        for i in range(1, NZ):
            total += r3[turn(z, i, NZ), h].astype(F32)
        g3[z, h] = total.astype(BF16)
    for i in far:
        b = turn(z, i, NZ)
        go("tiles", g3.at[z], g3.at[z], oner.at[2], device(x, y, b, core))

    def along(h, j):
        at, b = left.at[sub(h, 0, j)], turn(c2[h], j, NY)
        go("lines", at, at, a1r.at[h, 0, b], up(h))
        go("lines", at, at, a1r.at[h, 1, b], down(h))

    def arrive(h, side, j):
        at, b = left.at[sub(h, 3 if side == 0 else 1, j)], turn(c2[h], j, NY)
        landed(at, a1r.at[h, side, b])

    def relay(h, side, j):
        at, b = left.at[sub(h, 3 if side == 0 else 1, j)], turn(c2[h], j, NY)
        go("lines", at, at, axr.at[h, b], up(h) if side == 0 else down(h))

    def cross(h, i):
        at = left.at[rows(mine + line(h, i), LINE)]
        go("cross", at, at, oner.at[3], sibling)

    def across_rows(a, b):
        return lax.dot_general(a, b, (((0,), (0,)), ((), ())), preferred_element_type=F32)

    def products(h, i):
        part = left[rows(mine + line(h, i), LINE), :]
        gpart[h * NX + turn(c1[h], i, NX)] = across_rows(part, part)

    def far_line(h, j):
        at, b = left.at[sub(h, 2, j)], turn(c2[h], j, NY)
        landed(at, axr.at[h, b])

    landed(span(g3, NZ - 1), oner.at[2])
    for h in range(2):
        left[sub(h, 0, 0), :] = jnp.concatenate(
            [jnp.concatenate([g3[c * 4 + v, h] for c in range(2)], axis=1) for v in range(4)], axis=0
        )
        at = left.at[sub(h, 0, 0)]
        for i in (2, 1, 3):
            b = turn(c2[h], i, NY)
            go("gather", at, at, a2r.at[h, c2[h]], peer2(h, b))
        along(h, 0)
    for j in (1, 3, 2):
        for h in range(2):
            at, b = left.at[sub(h, 0, j)], turn(c2[h], j, NY)
            landed(at, a2r.at[h, b])
            along(h, j)
    for j, side in ((0, 0), (1, 0), (3, 1), (2, 1)):
        for h in range(2):
            arrive(h, side, j)
            relay(h, side, j)
    for h in range(2):
        cross(h, 0)

    owner = x * 2 + core
    others = [(turn(x, i, NX), lax.rem(core + e, 2)) for i in range(NX) for e in range(2) if i or e]

    def piece(v, c):
        return rows((v * 2 + c) * PIECE, PIECE)

    total = across_rows(left[rows(mine + line(0, 0), LINE), :], sx[0])
    landed(span(rx, NX - 1), oner.at[1])
    owned = xs[:, x].astype(F32)
    for i in range(1, NX):
        owned += rx[turn(x, i, NX)].astype(F32)
    sx[1] = owned.astype(BF16).reshape(LINE, RANK)
    arrive(1, 1, 0)
    far_line(1, 0)
    owned = jnp.concatenate([left[rows(mine + PART + v * LINE + x * SUB, SUB), :] for v in range(NY)], axis=0)
    zsum[...] = total + across_rows(owned, sx[1])
    zsend[...] = zsum[...].astype(BF16)
    for v, c in others:
        go("right", zsend.at[piece(v, c)], zr.at[owner], oner.at[5], device(v, y, z, c))

    for h in range(2):
        products(h, 0)
    for h in range(2):
        arrive(h, 0, 3)
        arrive(h, 0, 2)
        cross(h, 3)
        products(h, 3)
    for h in range(2):
        if h == 0:
            arrive(h, 1, 0)
        arrive(h, 1, 1)
        cross(h, 1)
        products(h, 1)
    for h in range(2):
        for j in (0, 1, 3, 2)[h:]:
            far_line(h, j)
        products(h, 2)

    total = gpart[0]
    for i in range(1, 2 * NX):
        total += gpart[i]
    gsum[...] = total
    go("gram", gsum, gin, oner.at[4], sibling)

    for h in range(2):
        cross(h, 2)
    across = device(x, y, turn(z, ZLO, NZ), core)

    def add_pieces():
        landed(span(zr, OWNERS - 1), oner.at[5])
        total = zsum[piece(x, core), :]
        for v, c in others:
            total += zr[v * 2 + c].astype(F32)
        zown[...] = total.astype(BF16)
        go("across", zown, zpair, oner.at[6], across)

    def add_across():
        landed(zpair, oner.at[6])
        here = piece(x, core)
        zall[here, :] = (zown[...].astype(F32) + zpair[...].astype(F32)).astype(BF16)
        for v, c in others:
            go("back", zall.at[here], zall.at[here], oner.at[7], device(v, y, z, c))

    add_pieces()
    sent("z", span(r3, NZ - 1))
    sent("merged", span(rx, NX - 1))
    sent("tiles", span(r3, NZ - 1))
    sent("gather", span(left, 6 * SUB))
    sent("lines", span(left, 24 * SUB))
    landed(gin, oner.at[4])
    inverse = inverse_factor(gsum[...] + gin[...], ({}, {3: add_across}))
    landed(span(zall, (OWNERS - 1) * PIECE), oner.at[7])
    w1 = inverse.astype(BF16)
    w2 = (inverse - w1.astype(F32)).astype(BF16)

    def apply(matrix, dim):
        dims = (((dim,), (0,)), ((), ()))
        return sum(lax.dot_general(w, matrix, dims, preferred_element_type=F32) for w in (w1, w2))

    factor = (apply(zall[...], 1) / PODS).astype(BF16)
    new_factor[...] = factor.T
    mix = apply(factor, 0)
    head = mix.astype(BF16)
    high[...] = head
    low[...] = (mix - head.astype(F32)).astype(BF16)

    landed(span(left, MINE), oner.at[3])
    load_momentum.wait()
    sent("cross", span(left, MINE))
    sent("gram", gsum)
    sent("right", span(zr, OWNERS - 1))
    sent("across", zown)
    sent("back", span(zr, OWNERS - 1))


def gather(delta, error, momentum, q):
    vmem, hbm = (pl.BlockSpec(memory_space=s) for s in (pltpu.VMEM, pltpu.HBM))
    dma = pltpu.SemaphoreType.DMA
    wide, square = (ROWS, RANK), (RANK, RANK)
    return pl.pallas_call(
        exchange,
        out_shape=(
            jax.ShapeDtypeStruct(wide, BF16),
            jax.ShapeDtypeStruct(wide, BF16),
            jax.ShapeDtypeStruct(wide, BF16),
            jax.ShapeDtypeStruct(square, BF16),
            jax.ShapeDtypeStruct(square, BF16),
            jax.ShapeDtypeStruct(square, BF16),
        ),
        in_specs=[hbm] * 4,
        out_specs=(vmem,) * 6,
        scratch_shapes=[
            pltpu.VMEM(square, BF16),
            pltpu.VMEM(wide, BF16),
            pltpu.VMEM(wide, BF16),
            pltpu.VMEM((MINE, RANK), BF16),
            pltpu.VMEM((MINE, RANK), BF16),
            pltpu.VMEM((NY, NX, SUB, RANK), BF16),
            pltpu.VMEM((NX, NY, SUB, RANK), BF16),
            pltpu.VMEM((2, LINE, RANK), BF16),
            pltpu.VMEM((2, 2, LINE // 2, RANK), F32),
            pltpu.VMEM((2, 2, LINE // 2, RANK), BF16),
            pltpu.VMEM((2, 2, LINE // 2, RANK), BF16),
            pltpu.VMEM((2, 2, LINE // 2, RANK), BF16),
            pltpu.VMEM((2, LINE, RANK), F32),
            pltpu.VMEM((2, LINE, RANK), BF16),
            pltpu.VMEM((2, NY, SUB, RANK), BF16),
            pltpu.VMEM((2, 2, SUB, HALF), BF16),
            pltpu.VMEM((NZ, 2, TILE, HALF), BF16),
            pltpu.VMEM((2, 2, SUB, HALF), F32),
            pltpu.VMEM((NZ, 2, TILE, HALF), BF16),
            pltpu.VMEM((2 * NX,) + square, F32),
            pltpu.VMEM(square, F32),
            pltpu.VMEM(square, F32),
            pltpu.VMEM(square, F32),
            pltpu.VMEM(square, BF16),
            pltpu.VMEM((OWNERS, PIECE, RANK), BF16),
            pltpu.VMEM((PIECE, RANK), BF16),
            pltpu.VMEM((PIECE, RANK), BF16),
            pltpu.VMEM(square, BF16),
            dma((10,)), dma((13,)), dma((NX,)), dma((2, 2)), dma((2,)), dma((2,)), dma((8,)),
            dma((2, NY)), dma((2, 2, NY)), dma((2, NY)),
        ],
        compiler_params=pltpu.CompilerParams(collective_id=0, has_side_effects=True, vmem_limit_bytes=32 << 20),
        cost_estimate=pl.CostEstimate(flops=6 * ROWS * RANK * RANK, bytes_accessed=5 * ROWS * RANK * 2, transcendentals=0),
        name="gather_left",
    )(*(pltpu.with_memory_space_constraint(a, pltpu.HBM) for a in (delta, error, momentum, q)))


def finish(left, merged, momentum, high, low, factor, new_error, new_momentum, outer_step, new_factor, e, m, s, sem):
    size, count = ROWS // 8, 8
    copies = [pltpu.make_async_copy(factor, new_factor, sem.at[count, 0])]
    copies[0].start()
    for i in range(count):
        at = pl.ds(i * size, size)
        block = left[at, :]
        approx = jnp.dot(block, high[...], preferred_element_type=F32) + jnp.dot(
            block, low[...], preferred_element_type=F32
        )
        e[at, :] = (merged[at, :].astype(F32) - approx).astype(BF16)
        moment = 0.9 * momentum[at, :].astype(F32) + approx
        m[at, :] = moment.astype(BF16)
        s[at, :] = (0.7 * (approx + 0.9 * moment)).astype(BF16)
        for k, (src, dst) in enumerate(((e, new_error.at[0, at]), (m, new_momentum.at[at]), (s, outer_step.at[at]))):
            copies.append(pltpu.make_async_copy(src.at[at], dst, sem.at[i, k]))
            copies[-1].start()
    for copy in copies:
        copy.wait()


def outputs(left, merged, momentum, high, low, factor):
    any_, vmem = pl.BlockSpec(memory_space=pl.ANY), pl.BlockSpec(memory_space=pltpu.VMEM)
    wide = (ROWS, RANK)
    return pl.pallas_call(
        finish,
        out_shape=(
            jax.ShapeDtypeStruct((1,) + wide, BF16),
            jax.ShapeDtypeStruct(wide, BF16),
            jax.ShapeDtypeStruct(wide, BF16),
            jax.ShapeDtypeStruct((RANK, RANK), BF16),
        ),
        in_specs=[vmem] * 6,
        out_specs=(any_,) * 4,
        scratch_shapes=[pltpu.VMEM(wide, BF16)] * 3 + [pltpu.SemaphoreType.DMA((9, 3))],
        compiler_params=pltpu.CompilerParams(vmem_limit_bytes=24 << 20),
        cost_estimate=pl.CostEstimate(flops=4 * ROWS * RANK * RANK, bytes_accessed=6 * ROWS * RANK * 2, transcendentals=0),
        name="outputs",
    )(left, merged, momentum, high, low, factor)


def body(delta, error, momentum, q_init):
    left, merged, held, high, low, factor = gather(delta, error, momentum, q_init)
    return outputs(left, merged, held, high, low, factor)


def solution(mesh):
    placed = (P("outer", None, "tp"), P("outer", None, "tp"), P(None, "tp"), P("tp", None))
    return jax.shard_map(
        body,
        mesh=mesh,
        in_specs=placed,
        out_specs=(P("outer", None, "tp"), P(None, "tp"), P(None, "tp"), P("tp", None)),
        check_vma=False,
    )
```

```python
import jax
import jax.numpy as jnp
from jax import lax
from jax.experimental import pallas as pl
from jax.experimental.pallas import tpu as pltpu
from jax.sharding import PartitionSpec as P

MESH = pl.DeviceIdType.MESH
F32, BF16 = jnp.float32, jnp.bfloat16
NX, NY, NZ, ZLO = 4, 4, 8, 4
ROWS, RANK, HALF = 4096, 256, 128
MINE = ROWS // 2
PART = MINE // 2
LINE = PART // NX
SUB = LINE // NY
TILE = 16
PODS = 16
OWNERS = 2 * NX
PIECE = RANK // OWNERS


HIGH = lax.Precision.HIGHEST


def mm(a, b, dims):
    return lax.dot_general(a, b, (dims, ((), ())), precision=HIGH, preferred_element_type=F32)


def reciprocal(d):
    return pltpu.reciprocal(d, approx=True)


def factor_block(a, between):
    tile = (8, 128)
    lane = lax.broadcasted_iota(jnp.int32, tile, 1)
    row = lax.broadcasted_iota(jnp.int32, tile, 0)
    tiles = a.reshape(16, 8, 128)
    both, rest = tiles[:2], tiles[2:]
    done = []
    for g in range(16):
        first = 8 * g
        shape = both.shape
        below = shape[0] - 1
        cols = [jnp.broadcast_to(both[:, :, first + c:first + c + 1], shape) for c in range(8)]
        here = (lane >= first) & (lane < first + 8)
        start = [jnp.where(here, jnp.where(lane - first == row, 1.0, 0.0), both[0])]
        start += [jnp.where(here, 0.0, both[1])] * below
        both = jnp.stack(start)
        diag = jnp.ones(tile, F32)

        def spread(x, r):
            return jnp.broadcast_to(x[0, r:r + 1], tile)

        def after(r, x):
            top = jnp.where(row > r, x[:1], 0.0)
            return jnp.concatenate([top, x[1:]], axis=0) if below else top

        for p in range(0, 8, 2):
            q = p + 1
            d_p, d_pq, d_q = spread(cols[p], p), spread(cols[p], q), spread(cols[q], q)
            det = d_p * d_q - d_pq * d_pq
            inv_p = reciprocal(d_p)
            inv_q = d_p * reciprocal(det)
            ratio = d_pq * inv_p
            line_p = spread(both, p)
            line_q = spread(both, q) - ratio * line_p
            diag = jnp.where(row == p, d_p, jnp.where(row == q, det * inv_p, diag))
            part_p = after(p, cols[p] * inv_p)
            part_q = after(q, (cols[q] - part_p * d_pq) * inv_q)
            both = both - part_p * line_p - part_q * line_q
            for k in range(q + 1, 8):
                edge_p = spread(cols[k], p)
                edge_q = spread(cols[k], q) - ratio * edge_p
                cols[k] = cols[k] - part_p * edge_p - part_q * edge_q
        upper = both[0]
        done.append(jnp.where(lane <= row + first, upper * (1.0 / jnp.sqrt(diag)), 0.0))
        if g < 14:
            factors = (upper / diag).T[first + 16:].reshape(rest.shape[0], 8, 8)
            rest = jnp.where(here, 0.0, rest)
            for c in range(8):
                rest = rest - factors[:, :, c:c + 1] * upper[c:c + 1]
            both = jnp.concatenate([both[1:], rest[:1]], axis=0)
            rest = rest[1:] if g < 13 else None
        elif g < 15:
            both = both[1:]
        if g in between:
            between[g]()
    return jnp.concatenate(done, axis=0)


def inverse_factor(gram, between):
    on = lax.broadcasted_iota(jnp.int32, gram.shape, 0) == lax.broadcasted_iota(jnp.int32, gram.shape, 1)
    diagonal = jnp.where(on, gram, 0.0)
    scale = 1.0 / jnp.sqrt(jnp.sum(diagonal, axis=0, keepdims=True))
    gram = gram * scale * (1.0 / jnp.sqrt(jnp.sum(diagonal, axis=1, keepdims=True)))
    w11 = factor_block(gram[:128, :128], between[0])
    l21 = mm(gram[128:, :128], w11, ((1,), (1,)))
    w22 = factor_block(gram[128:, 128:] - mm(l21, l21, ((1,), (1,))), between[1])
    w21 = -mm(w22, mm(l21, w11, ((1,), (0,))), ((1,), (0,)))
    top = jnp.concatenate([w11, jnp.zeros((128, 128), F32)], axis=1)
    return jnp.concatenate([top, jnp.concatenate([w21, w22], axis=1)], axis=0) * scale


def device(x, y, z, core):
    return ((z // ZLO) * NX + x) * 2 + core, (z % ZLO) * NY + y


def send(src, dst, send_sem, recv_sem, dev):
    return pltpu.make_async_remote_copy(
        src_ref=src, dst_ref=dst, send_sem=send_sem, recv_sem=recv_sem, device_id=dev, device_id_type=MESH
    )


def exchange(
    delta, error, momentum, q_in, left, merged, held, high, low, new_factor,
    q, dbuf, ebuf, pair_in, s1, xs, rx, sx, r1, o1, s2, r2, s3, r3, o3, g3,
    gpart, gsum, gin, zsum, zsend, zr, zown, zpair, zall,
    ld, ss, cr, p1r, p2r, oner, a2r, a1r,
):
    o, t = lax.axis_index("outer"), lax.axis_index("tp")
    core, x, y = lax.rem(o, 2), lax.rem(o // 2, NX), lax.rem(t, NY)
    z = (o // (2 * NX)) * ZLO + t // NY
    sibling = device(x, y, z, 1 - core)
    c1, c2 = (x, y), (y, x)

    def peer1(h, v):
        return device(v, y, z, core) if h == 0 else device(x, v, z, core)

    def peer2(h, v):
        return device(x, v, z, core) if h == 0 else device(v, y, z, core)

    def turn(v, i, n):
        return lax.rem(v + i, n)

    def rows(start, size):
        return pl.ds(pl.multiple_of(start, TILE), size)

    mine, theirs = core * MINE, (1 - core) * MINE

    def line(h, i):
        return h * PART + turn(c1[h], i, NX) * LINE

    order = [(whose, i) for whose in range(2) for i in (2, 1, 3, 0)]

    def loads(whose, i, h):
        src, k = rows((mine if whose else theirs) + line(h, i), LINE), whose * NX + i
        return (
            pltpu.make_async_copy(delta.at[0, src], dbuf.at[src], ld.at[k]),
            pltpu.make_async_copy(error.at[0, src], ebuf.at[src], ld.at[k]),
        )

    barrier = pltpu.get_barrier_semaphore()
    greeted = [sibling]
    greeted += [device(turn(x, i, NX), y, z, core) for i in range(1, NX)]
    greeted += [device(x, turn(y, i, NY), z, core) for i in range(1, NY)]
    greeted += [device(x, y, turn(z, i, NZ), core) for i in range(1, NZ)]
    greeted += [device(turn(x, i, NX), y, z, 1 - core) for i in range(1, NX)]
    for dev in greeted:
        pl.semaphore_signal(barrier, inc=1, device_id=dev, device_id_type=MESH)

    for whose, i in order:
        for h in range(2):
            for copy in loads(whose, i, h):
                copy.start()
    load_q = pltpu.make_async_copy(q_in, q, ld.at[8])
    load_q.start()

    stages = ("core", "first", "second", "z", "merged", "tiles", "gather", "lines", "cross", "gram", "right", "across", "back")

    def go(stage, src, dst, recv_sem, dev):
        send(src, dst, ss.at[stages.index(stage)], recv_sem, dev).start()

    def sent(stage, ref):
        sem = ss.at[stages.index(stage)]
        send(ref, ref, sem, sem, sibling).wait_send()

    def landed(ref, sem):
        send(ref, ref, ss.at[0], sem, sibling).wait_recv()

    def span(ref, size):
        return ref.at[pl.ds(0, size)]

    def merge(whose, i, h):
        if h == 0:
            every = span(dbuf, 4 * LINE)
            pltpu.make_async_copy(every, every, ld.at[whose * NX + i]).wait()
        block = rows((mine if whose else theirs) + line(h, i), LINE)
        total = (dbuf[block, :].astype(F32) + ebuf[block, :].astype(F32)).astype(BF16)
        merged[block, :] = total
        return block, total.astype(F32)

    def give(i, h):
        block, _ = merge(0, i, h)
        here = rows(line(h, i), LINE)
        go("core", merged.at[block], pair_in.at[here], cr.at[i], sibling)

    def take(i, h):
        _, total = merge(1, i, h)
        at = line(h, i)
        here = rows(at, LINE)
        if h == 0:
            landed(span(pair_in, 2 * LINE), cr.at[i])
        total = total + pair_in[here, :].astype(F32)
        if h == 1:
            both = total.astype(BF16)
            xs[turn(y, i, NY)] = both.reshape(NX, SUB, RANK)
            total = jnp.dot(both, q[...], preferred_element_type=F32)
        if i:
            s1[here, :] = total.astype(BF16)
            go("first", s1.at[here], r1.at[h, c1[h]], p1r.at[h], peer1(h, turn(c1[h], i, NX)))
        else:
            o1[h] = total

    for n, (whose, i) in enumerate(order):
        if n == 0:
            pl.semaphore_wait(barrier, len(greeted))
        if n == 2:
            load_q.wait()
        for h in range(2):
            if whose:
                take(i, h)
            else:
                give(i, h)

    load_momentum = pltpu.make_async_copy(momentum, held, ld.at[9])
    load_momentum.start()

    for h in range(2):
        landed(span(s1, 3 * LINE), p1r.at[h])
        total = o1[h]
        for i in range(1, NX):
            total += r1[h, turn(c1[h], i, NX)].astype(F32)
        o1[h] = total
        if h == 0:
            sx[0] = o1[0].astype(BF16)
            o1[0] = jnp.dot(sx[0], q[...], preferred_element_type=F32)
        s2[h] = o1[h].astype(BF16)
        for i in (2, 1, 3):
            b = turn(c2[h], i, NY)
            go("second", s2.at[h, rows(b * SUB, SUB)], r2.at[h, c2[h]], p2r.at[h], peer2(h, b))
    for h in range(2):
        landed(r2.at[h, pl.ds(0, NY - 1)], p2r.at[h])
        total = o1[h, rows(c2[h] * SUB, SUB), :]
        for i in range(1, NY):
            total += r2[h, turn(c2[h], i, NY)].astype(F32)
        for c in range(2):
            o3[h, c] = total[:, c * HALF:(c + 1) * HALF]
            s3[h, c] = total[:, c * HALF:(c + 1) * HALF].astype(BF16)

    far = (4, 3, 5, 2, 6, 1, 7)

    def spot(v):
        return v // 4, rows((v % 4) * TILE, TILE)

    for i in far:
        b = turn(z, i, NZ)
        c, at = spot(b)
        go("z", s3.at[:, c, at], r3.at[z], oner.at[0], device(x, y, b, core))
    for i in (2, 1, 3):
        b = turn(x, i, NX)
        go("merged", xs.at[:, b], rx.at[x], oner.at[1], device(b, y, z, core))
    sent("core", span(left, 2 * PART))
    sent("first", span(left, 6 * LINE))
    sent("second", span(left, 6 * SUB))
    landed(span(r3, NZ - 1), oner.at[0])

    def sub(h, i, j):
        return rows(mine + line(h, i) + turn(c2[h], j, NY) * SUB, SUB)

    c, at = spot(z)
    for h in range(2):
        total = o3[h, c, at, :]
        for i in range(1, NZ):
            total += r3[turn(z, i, NZ), h].astype(F32)
        g3[z, h] = total.astype(BF16)
    for i in far:
        b = turn(z, i, NZ)
        go("tiles", g3.at[z], g3.at[z], oner.at[2], device(x, y, b, core))

    def along(h, j):
        at, b = left.at[sub(h, 0, j)], turn(c2[h], j, NY)
        for i in (2, 1, 3):
            go("lines", at, at, a1r.at[h, c1[h], b], peer1(h, turn(c1[h], i, NX)))

    def arrive(h, i, j):
        landed(left.at[sub(h, i, j)], a1r.at[h, turn(c1[h], i, NX), turn(c2[h], j, NY)])

    def cross(h, i):
        at = left.at[rows(mine + line(h, i), LINE)]
        go("cross", at, at, oner.at[3], sibling)

    def across_rows(a, b):
        return lax.dot_general(a, b, (((0,), (0,)), ((), ())), preferred_element_type=F32)

    def products(h, i):
        part = left[rows(mine + line(h, i), LINE), :]
        gpart[h * NX + turn(c1[h], i, NX)] = across_rows(part, part)

    landed(span(g3, NZ - 1), oner.at[2])
    for h in range(2):
        left[sub(h, 0, 0), :] = jnp.concatenate(
            [jnp.concatenate([g3[c * 4 + v, h] for c in range(2)], axis=1) for v in range(4)], axis=0
        )
        at = left.at[sub(h, 0, 0)]
        for i in (2, 1, 3):
            b = turn(c2[h], i, NY)
            go("gather", at, at, a2r.at[h, c2[h]], peer2(h, b))
        along(h, 0)
    for j in (1, 3, 2):
        for h in range(2):
            at, b = left.at[sub(h, 0, j)], turn(c2[h], j, NY)
            landed(at, a2r.at[h, b])
            along(h, j)
    for h in range(2):
        cross(h, 0)

    owner = x * 2 + core
    others = [(turn(x, i, NX), lax.rem(core + e, 2)) for i in range(NX) for e in range(2) if i or e]

    def piece(v, c):
        return rows((v * 2 + c) * PIECE, PIECE)

    total = across_rows(left[rows(mine + line(0, 0), LINE), :], sx[0])
    landed(span(rx, NX - 1), oner.at[1])
    owned = xs[:, x].astype(F32)
    for i in range(1, NX):
        owned += rx[turn(x, i, NX)].astype(F32)
    sx[1] = owned.astype(BF16).reshape(LINE, RANK)
    for i in (1, 3, 2):
        arrive(1, i, 0)
    owned = jnp.concatenate([left[rows(mine + PART + v * LINE + x * SUB, SUB), :] for v in range(NY)], axis=0)
    zsum[...] = total + across_rows(owned, sx[1])
    zsend[...] = zsum[...].astype(BF16)
    for v, c in others:
        go("right", zsend.at[piece(v, c)], zr.at[owner], oner.at[5], device(v, y, z, c))

    for h in range(2):
        products(h, 0)
    for i in (1, 3, 2):
        for h in range(2):
            for j in (0, 1, 3, 2)[h:]:
                arrive(h, i, j)
            if i != 2:
                cross(h, i)
            products(h, i)

    total = gpart[0]
    for i in range(1, 2 * NX):
        total += gpart[i]
    gsum[...] = total
    go("gram", gsum, gin, oner.at[4], sibling)

    for h in range(2):
        cross(h, 2)
    across = device(x, y, turn(z, ZLO, NZ), core)

    def add_pieces():
        landed(span(zr, OWNERS - 1), oner.at[5])
        total = zsum[piece(x, core), :]
        for v, c in others:
            total += zr[v * 2 + c].astype(F32)
        zown[...] = total.astype(BF16)
        go("across", zown, zpair, oner.at[6], across)

    def add_across():
        landed(zpair, oner.at[6])
        here = piece(x, core)
        zall[here, :] = (zown[...].astype(F32) + zpair[...].astype(F32)).astype(BF16)
        for v, c in others:
            go("back", zall.at[here], zall.at[here], oner.at[7], device(v, y, z, c))

    add_pieces()
    sent("z", span(r3, NZ - 1))
    sent("merged", span(rx, NX - 1))
    sent("tiles", span(r3, NZ - 1))
    sent("gather", span(left, 6 * SUB))
    sent("lines", span(left, 24 * SUB))
    landed(gin, oner.at[4])
    inverse = inverse_factor(gsum[...] + gin[...], ({}, {3: add_across}))
    landed(span(zall, (OWNERS - 1) * PIECE), oner.at[7])
    w1 = inverse.astype(BF16)
    w2 = (inverse - w1.astype(F32)).astype(BF16)

    def apply(matrix, dim):
        dims = (((dim,), (0,)), ((), ()))
        return sum(lax.dot_general(w, matrix, dims, preferred_element_type=F32) for w in (w1, w2))

    factor = (apply(zall[...], 1) / PODS).astype(BF16)
    new_factor[...] = factor.T
    mix = apply(factor, 0)
    head = mix.astype(BF16)
    high[...] = head
    low[...] = (mix - head.astype(F32)).astype(BF16)

    landed(span(left, MINE), oner.at[3])
    load_momentum.wait()
    sent("cross", span(left, MINE))
    sent("gram", gsum)
    sent("right", span(zr, OWNERS - 1))
    sent("across", zown)
    sent("back", span(zr, OWNERS - 1))


def gather(delta, error, momentum, q):
    vmem, hbm = (pl.BlockSpec(memory_space=s) for s in (pltpu.VMEM, pltpu.HBM))
    dma = pltpu.SemaphoreType.DMA
    wide, square = (ROWS, RANK), (RANK, RANK)
    return pl.pallas_call(
        exchange,
        out_shape=(
            jax.ShapeDtypeStruct(wide, BF16),
            jax.ShapeDtypeStruct(wide, BF16),
            jax.ShapeDtypeStruct(wide, BF16),
            jax.ShapeDtypeStruct(square, BF16),
            jax.ShapeDtypeStruct(square, BF16),
            jax.ShapeDtypeStruct(square, BF16),
        ),
        in_specs=[hbm] * 4,
        out_specs=(vmem,) * 6,
        scratch_shapes=[
            pltpu.VMEM(square, BF16),
            pltpu.VMEM(wide, BF16),
            pltpu.VMEM(wide, BF16),
            pltpu.VMEM((MINE, RANK), BF16),
            pltpu.VMEM((MINE, RANK), BF16),
            pltpu.VMEM((NY, NX, SUB, RANK), BF16),
            pltpu.VMEM((NX, NY, SUB, RANK), BF16),
            pltpu.VMEM((2, LINE, RANK), BF16),
            pltpu.VMEM((2, NX, LINE, RANK), BF16),
            pltpu.VMEM((2, LINE, RANK), F32),
            pltpu.VMEM((2, LINE, RANK), BF16),
            pltpu.VMEM((2, NY, SUB, RANK), BF16),
            pltpu.VMEM((2, 2, SUB, HALF), BF16),
            pltpu.VMEM((NZ, 2, TILE, HALF), BF16),
            pltpu.VMEM((2, 2, SUB, HALF), F32),
            pltpu.VMEM((NZ, 2, TILE, HALF), BF16),
            pltpu.VMEM((2 * NX,) + square, F32),
            pltpu.VMEM(square, F32),
            pltpu.VMEM(square, F32),
            pltpu.VMEM(square, F32),
            pltpu.VMEM(square, BF16),
            pltpu.VMEM((OWNERS, PIECE, RANK), BF16),
            pltpu.VMEM((PIECE, RANK), BF16),
            pltpu.VMEM((PIECE, RANK), BF16),
            pltpu.VMEM(square, BF16),
            dma((10,)), dma((13,)), dma((NX,)), dma((2,)), dma((2,)), dma((8,)), dma((2, NY)), dma((2, NX, NY)),
        ],
        compiler_params=pltpu.CompilerParams(collective_id=0, has_side_effects=True, vmem_limit_bytes=32 << 20),
        cost_estimate=pl.CostEstimate(flops=6 * ROWS * RANK * RANK, bytes_accessed=5 * ROWS * RANK * 2, transcendentals=0),
        name="gather_left",
    )(*(pltpu.with_memory_space_constraint(a, pltpu.HBM) for a in (delta, error, momentum, q)))


def finish(left, merged, momentum, high, low, factor, new_error, new_momentum, outer_step, new_factor, e, m, s, sem):
    size, count = ROWS // 8, 8
    copies = [pltpu.make_async_copy(factor, new_factor, sem.at[count, 0])]
    copies[0].start()
    for i in range(count):
        at = pl.ds(i * size, size)
        block = left[at, :]
        approx = jnp.dot(block, high[...], preferred_element_type=F32) + jnp.dot(
            block, low[...], preferred_element_type=F32
        )
        e[at, :] = (merged[at, :].astype(F32) - approx).astype(BF16)
        moment = 0.9 * momentum[at, :].astype(F32) + approx
        m[at, :] = moment.astype(BF16)
        s[at, :] = (0.7 * (approx + 0.9 * moment)).astype(BF16)
        for k, (src, dst) in enumerate(((e, new_error.at[0, at]), (m, new_momentum.at[at]), (s, outer_step.at[at]))):
            copies.append(pltpu.make_async_copy(src.at[at], dst, sem.at[i, k]))
            copies[-1].start()
    for copy in copies:
        copy.wait()


def outputs(left, merged, momentum, high, low, factor):
    any_, vmem = pl.BlockSpec(memory_space=pl.ANY), pl.BlockSpec(memory_space=pltpu.VMEM)
    wide = (ROWS, RANK)
    return pl.pallas_call(
        finish,
        out_shape=(
            jax.ShapeDtypeStruct((1,) + wide, BF16),
            jax.ShapeDtypeStruct(wide, BF16),
            jax.ShapeDtypeStruct(wide, BF16),
            jax.ShapeDtypeStruct((RANK, RANK), BF16),
        ),
        in_specs=[vmem] * 6,
        out_specs=(any_,) * 4,
        scratch_shapes=[pltpu.VMEM(wide, BF16)] * 3 + [pltpu.SemaphoreType.DMA((9, 3))],
        compiler_params=pltpu.CompilerParams(vmem_limit_bytes=24 << 20),
        cost_estimate=pl.CostEstimate(flops=4 * ROWS * RANK * RANK, bytes_accessed=6 * ROWS * RANK * 2, transcendentals=0),
        name="outputs",
    )(left, merged, momentum, high, low, factor)


def body(delta, error, momentum, q_init):
    left, merged, held, high, low, factor = gather(delta, error, momentum, q_init)
    return outputs(left, merged, held, high, low, factor)


def solution(mesh):
    placed = (P("outer", None, "tp"), P("outer", None, "tp"), P(None, "tp"), P("tp", None))
    return jax.shard_map(
        body,
        mesh=mesh,
        in_specs=placed,
        out_specs=(P("outer", None, "tp"), P(None, "tp"), P(None, "tp"), P("tp", None)),
        check_vma=False,
    )
```

```python
import jax
import jax.numpy as jnp
from jax import lax
from jax.experimental import pallas as pl
from jax.experimental.pallas import tpu as pltpu
from jax.sharding import PartitionSpec as P

MESH = pl.DeviceIdType.MESH
F32, BF16 = jnp.float32, jnp.bfloat16
NX, NY, NZ, ZLO = 4, 4, 8, 4
ROWS, RANK, HALF = 4096, 256, 128
MINE = ROWS // 2
PART = MINE // 2
LINE = PART // NX
SUB = LINE // NY
TILE = 16
PODS = 16
OWNERS = 2 * NX
PIECE = RANK // OWNERS


HIGH = lax.Precision.HIGHEST


def mm(a, b, dims):
    return lax.dot_general(a, b, (dims, ((), ())), precision=HIGH, preferred_element_type=F32)


def reciprocal(d):
    return pltpu.reciprocal(d, approx=True)


def factor_block(a, between):
    tile = (8, 128)
    lane = lax.broadcasted_iota(jnp.int32, tile, 1)
    row = lax.broadcasted_iota(jnp.int32, tile, 0)
    tiles = a.reshape(16, 8, 128)
    pivots, following, rest = tiles[0], tiles[1], tiles[2:]
    done = []
    for g in range(16):
        first = 8 * g
        here = (lane >= first) & (lane < first + 8)

        def column(x, c):
            return jnp.broadcast_to(x[:, first + c:first + c + 1], tile)

        def line(x, r):
            return jnp.broadcast_to(x[r:r + 1], tile)

        lefts = [column(pivots, c) for c in range(8)]
        block = {(r, c): line(lefts[c], r) for c in range(8) for r in range(c, 8)}
        own = jnp.where(here, jnp.where(lane - first == row, 1.0, 0.0), pivots)
        lines = [line(own, r) for r in range(8)]
        if g < 15:
            below = [column(following, c) for c in range(8)]
            following = jnp.where(here, 0.0, following)
        diag = jnp.ones(tile, F32)
        upper = own
        inverses = []
        for p in range(0, 8, 2):
            q = p + 1
            d_p, d_pq, d_q = block[p, p], block[q, p], block[q, q]
            det = d_p * d_q - d_pq * d_pq
            inv_p = reciprocal(d_p)
            inv_q = d_p * reciprocal(det)
            ratio = d_pq * inv_p
            inverses += [inv_p, inv_q]
            lines[q] = lines[q] - ratio * lines[p]
            diag = jnp.where(row == p, d_p, jnp.where(row == q, det * inv_p, diag))
            upper = jnp.where(row == q, lines[q], upper)
            later = range(q + 1, 8)
            edge_p = {k: block[k, p] for k in later}
            edge_q = {k: block[k, q] - ratio * edge_p[k] for k in later}
            part_p = {k: edge_p[k] * inv_p for k in later}
            part_q = {k: edge_q[k] * inv_q for k in later}
            for c in later:
                for r in range(c, 8):
                    block[r, c] = block[r, c] - part_p[r] * edge_p[c] - part_q[r] * edge_q[c]
            for k in later:
                lines[k] = lines[k] - part_p[k] * lines[p] - part_q[k] * lines[q]
                upper = jnp.where(row == k, lines[k], upper) if k == q + 1 else upper
            if g < 15:
                below_p = below[p] * inv_p
                below_q = (below[q] - below_p * d_pq) * inv_q
                following = following - below_p * lines[p] - below_q * lines[q]
                for k in later:
                    below[k] = below[k] - below_p * edge_p[k] - below_q * edge_q[k]
        done.append(jnp.where(lane <= row + first, upper * (1.0 / jnp.sqrt(diag)), 0.0))
        if g < 14:
            factors = (upper / diag).T[first + 16:].reshape(rest.shape[0], 8, 8)
            rest = jnp.where(here, 0.0, rest)
            for c in range(8):
                rest = rest - factors[:, :, c:c + 1] * lines[c]
            pivots, following, rest = following, rest[0], rest[1:] if g < 13 else None
        elif g == 14:
            pivots = following
        if g in between:
            between[g]()
    return jnp.concatenate(done, axis=0)


def inverse_factor(gram, between):
    on = lax.broadcasted_iota(jnp.int32, gram.shape, 0) == lax.broadcasted_iota(jnp.int32, gram.shape, 1)
    diagonal = jnp.where(on, gram, 0.0)
    scale = 1.0 / jnp.sqrt(jnp.sum(diagonal, axis=0, keepdims=True))
    gram = gram * scale * (1.0 / jnp.sqrt(jnp.sum(diagonal, axis=1, keepdims=True)))
    w11 = factor_block(gram[:128, :128], between[0])
    l21 = mm(gram[128:, :128], w11, ((1,), (1,)))
    corner = mm(l21, w11, ((1,), (0,)))
    w22 = factor_block(gram[128:, 128:] - mm(l21, l21, ((1,), (1,))), between[1])
    w21 = -mm(w22, corner, ((1,), (0,)))
    top = jnp.concatenate([w11, jnp.zeros((128, 128), F32)], axis=1)
    return jnp.concatenate([top, jnp.concatenate([w21, w22], axis=1)], axis=0) * scale


def device(x, y, z, core):
    return ((z // ZLO) * NX + x) * 2 + core, (z % ZLO) * NY + y


def send(src, dst, send_sem, recv_sem, dev):
    return pltpu.make_async_remote_copy(
        src_ref=src, dst_ref=dst, send_sem=send_sem, recv_sem=recv_sem, device_id=dev, device_id_type=MESH
    )


def exchange(
    delta, error, momentum, q_in, left, merged, held, mixed, new_factor,
    q, dbuf, ebuf, pair_in, s1, xs, rx, sx, r1, o1, o2, s2, r2, s3, r3, o3, g3,
    gpart, gsum, gin, zsum, zsend, zr, zown, zpair, zall,
    ld, ss, cr, p1r, p2r, oner, a2r, a1r,
):
    o, t = lax.axis_index("outer"), lax.axis_index("tp")
    core, x, y = lax.rem(o, 2), lax.rem(o // 2, NX), lax.rem(t, NY)
    z = (o // (2 * NX)) * ZLO + t // NY
    sibling = device(x, y, z, 1 - core)
    c1, c2 = (x, y), (y, x)

    def peer1(h, v):
        return device(v, y, z, core) if h == 0 else device(x, v, z, core)

    def peer2(h, v):
        return device(x, v, z, core) if h == 0 else device(v, y, z, core)

    def turn(v, i, n):
        return lax.rem(v + i, n)

    def rows(start, size):
        return pl.ds(pl.multiple_of(start, TILE), size)

    mine, theirs = core * MINE, (1 - core) * MINE

    def line(h, i):
        return h * PART + turn(c1[h], i, NX) * LINE

    order = [(whose, i) for whose in range(2) for i in (2, 1, 3, 0)]

    def loads(whose, i, h):
        src, k = rows((mine if whose else theirs) + line(h, i), LINE), whose * NX + i
        return (
            pltpu.make_async_copy(delta.at[0, src], dbuf.at[src], ld.at[k]),
            pltpu.make_async_copy(error.at[0, src], ebuf.at[src], ld.at[k]),
        )

    def fetch(part):
        for whose, i in part:
            for h in range(2):
                for copy in loads(whose, i, h):
                    copy.start()

    fetch(order[:2])
    barrier = pltpu.get_barrier_semaphore()
    greeted = [sibling]
    greeted += [device(turn(x, i, NX), y, z, core) for i in range(1, NX)]
    greeted += [device(x, turn(y, i, NY), z, core) for i in range(1, NY)]
    greeted += [device(x, y, turn(z, i, NZ), core) for i in range(1, NZ)]
    greeted += [device(turn(x, i, NX), y, z, 1 - core) for i in range(1, NX)]
    for dev in greeted:
        pl.semaphore_signal(barrier, inc=1, device_id=dev, device_id_type=MESH)

    fetch(order[2:])
    load_q = pltpu.make_async_copy(q_in, q, ld.at[8])
    load_q.start()

    stages = ("core", "first", "second", "z", "merged", "tiles", "gather", "lines", "cross", "gram", "right", "across", "back")

    def go(stage, src, dst, recv_sem, dev):
        send(src, dst, ss.at[stages.index(stage)], recv_sem, dev).start()

    def sent(stage, ref):
        sem = ss.at[stages.index(stage)]
        send(ref, ref, sem, sem, sibling).wait_send()

    def landed(ref, sem):
        send(ref, ref, ss.at[0], sem, sibling).wait_recv()

    def span(ref, size):
        return ref.at[pl.ds(0, size)]

    def merge(whose, i, h):
        if h == 0:
            every = span(dbuf, 4 * LINE)
            pltpu.make_async_copy(every, every, ld.at[whose * NX + i]).wait()
        block = rows((mine if whose else theirs) + line(h, i), LINE)
        total = (dbuf[block, :].astype(F32) + ebuf[block, :].astype(F32)).astype(BF16)
        merged[block, :] = total
        return block, total.astype(F32)

    def give(i, h):
        block, _ = merge(0, i, h)
        here = rows(line(h, i), LINE)
        go("core", merged.at[block], pair_in.at[here], cr.at[i], sibling)

    def take(i, h):
        _, total = merge(1, i, h)
        at = line(h, i)
        here = rows(at, LINE)
        if h == 0:
            landed(span(pair_in, 2 * LINE), cr.at[i])
        total = total + pair_in[here, :].astype(F32)
        if h == 1:
            both = total.astype(BF16)
            xs[turn(y, i, NY)] = both.reshape(NX, SUB, RANK)
            total = jnp.dot(both, q[...], preferred_element_type=F32)
        if i:
            s1[here, :] = total.astype(BF16)
            go("first", s1.at[here], r1.at[h, c1[h]], p1r.at[h], peer1(h, turn(c1[h], i, NX)))
        else:
            o1[h] = total

    for n, (whose, i) in enumerate(order):
        if n == 0:
            pl.semaphore_wait(barrier, len(greeted))
        if n == 2:
            load_q.wait()
        for h in range(2):
            if whose:
                take(i, h)
            else:
                give(i, h)

    load_momentum = pltpu.make_async_copy(momentum, held, ld.at[9])
    load_momentum.start()

    for h in range(2):
        landed(span(s1, 3 * LINE), p1r.at[h])
        for i in (2, 1, 3, 0):
            b = turn(c2[h], i, NY)
            at = rows(b * SUB, SUB)
            total = o1[h, at, :]
            for j in range(1, NX):
                total += r1[h, turn(c1[h], j, NX), at, :].astype(F32)
            if h == 0:
                both = total.astype(BF16)
                sx[0, at, :] = both
                total = jnp.dot(both, q[...], preferred_element_type=F32)
            if i:
                s2[h, at, :] = total.astype(BF16)
                go("second", s2.at[h, at], r2.at[h, c2[h]], p2r.at[h], peer2(h, b))
            else:
                o2[h] = total
    for h in range(2):
        landed(r2.at[h, pl.ds(0, NY - 1)], p2r.at[h])
        total = o2[h]
        for i in range(1, NY):
            total += r2[h, turn(c2[h], i, NY)].astype(F32)
        for c in range(2):
            o3[h, c] = total[:, c * HALF:(c + 1) * HALF]
            s3[h, c] = total[:, c * HALF:(c + 1) * HALF].astype(BF16)

    far = (4, 3, 5, 2, 6, 1, 7)

    def spot(v):
        return v // 4, rows((v % 4) * TILE, TILE)

    for i in far:
        b = turn(z, i, NZ)
        c, at = spot(b)
        go("z", s3.at[:, c, at], r3.at[z], oner.at[0], device(x, y, b, core))
    for i in (2, 1, 3):
        b = turn(x, i, NX)
        go("merged", xs.at[:, b], rx.at[x], oner.at[1], device(b, y, z, core))
    sent("core", span(left, 2 * PART))
    sent("first", span(left, 6 * LINE))
    sent("second", span(left, 6 * SUB))
    landed(span(r3, NZ - 1), oner.at[0])

    def sub(h, i, j):
        return rows(mine + line(h, i) + turn(c2[h], j, NY) * SUB, SUB)

    c, at = spot(z)
    for h in range(2):
        total = o3[h, c, at, :]
        for i in range(1, NZ):
            total += r3[turn(z, i, NZ), h].astype(F32)
        g3[z, h] = total.astype(BF16)
    for i in far:
        b = turn(z, i, NZ)
        go("tiles", g3.at[z], g3.at[z], oner.at[2], device(x, y, b, core))

    def along(h, j):
        at, b = left.at[sub(h, 0, j)], turn(c2[h], j, NY)
        for i in (2, 1, 3):
            go("lines", at, at, a1r.at[h, c1[h], b], peer1(h, turn(c1[h], i, NX)))

    def arrive(h, i, j):
        landed(left.at[sub(h, i, j)], a1r.at[h, turn(c1[h], i, NX), turn(c2[h], j, NY)])

    def cross(h, i):
        at = left.at[rows(mine + line(h, i), LINE)]
        go("cross", at, at, oner.at[3], sibling)

    def across_rows(a, b):
        return lax.dot_general(a, b, (((0,), (0,)), ((), ())), preferred_element_type=F32)

    def products(h, i):
        part = left[rows(mine + line(h, i), LINE), :]
        gpart[h * NX + turn(c1[h], i, NX)] = across_rows(part, part)

    landed(span(g3, NZ - 1), oner.at[2])
    for h in range(2):
        left[sub(h, 0, 0), :] = jnp.concatenate(
            [jnp.concatenate([g3[c * 4 + v, h] for c in range(2)], axis=1) for v in range(4)], axis=0
        )
        at = left.at[sub(h, 0, 0)]
        for i in (2, 1, 3):
            b = turn(c2[h], i, NY)
            go("gather", at, at, a2r.at[h, c2[h]], peer2(h, b))
        along(h, 0)
    landed(span(rx, NX - 1), oner.at[1])
    owned = xs[:, x].astype(F32)
    for i in range(1, NX):
        owned += rx[turn(x, i, NX)].astype(F32)
    sx[1] = owned.astype(BF16).reshape(LINE, RANK)
    for j in (1, 3, 2):
        for h in range(2):
            at, b = left.at[sub(h, 0, j)], turn(c2[h], j, NY)
            landed(at, a2r.at[h, b])
            along(h, j)
    for h in range(2):
        cross(h, 0)

    owner = x * 2 + core
    others = [(turn(x, i, NX), lax.rem(core + e, 2)) for i in range(NX) for e in range(2) if i or e]

    def piece(v, c):
        return rows((v * 2 + c) * PIECE, PIECE)

    total = across_rows(left[rows(mine + line(0, 0), LINE), :], sx[0])
    for i in (1, 3, 2):
        arrive(1, i, 0)
    owned = jnp.concatenate([left[rows(mine + PART + v * LINE + x * SUB, SUB), :] for v in range(NY)], axis=0)
    zsum[...] = total + across_rows(owned, sx[1])
    zsend[...] = zsum[...].astype(BF16)
    for v, c in others:
        go("right", zsend.at[piece(v, c)], zr.at[owner], oner.at[5], device(v, y, z, c))

    for h in range(2):
        products(h, 0)
    for i in (1, 3, 2):
        for h in range(2):
            for j in (0, 1, 3, 2)[h:]:
                arrive(h, i, j)
            if i != 2:
                cross(h, i)
            products(h, i)

    total = gpart[0]
    for i in range(1, 2 * NX):
        total += gpart[i]
    gsum[...] = total
    go("gram", gsum, gin, oner.at[4], sibling)

    for h in range(2):
        cross(h, 2)
    across = device(x, y, turn(z, ZLO, NZ), core)

    def add_pieces():
        landed(span(zr, OWNERS - 1), oner.at[5])
        total = zsum[piece(x, core), :]
        for v, c in others:
            total += zr[v * 2 + c].astype(F32)
        zown[...] = total.astype(BF16)
        go("across", zown, zpair, oner.at[6], across)

    def add_across():
        landed(zpair, oner.at[6])
        here = piece(x, core)
        zall[here, :] = (zown[...].astype(F32) + zpair[...].astype(F32)).astype(BF16)
        for v, c in others:
            go("back", zall.at[here], zall.at[here], oner.at[7], device(v, y, z, c))

    add_pieces()
    sent("z", span(r3, NZ - 1))
    sent("merged", span(rx, NX - 1))
    sent("tiles", span(r3, NZ - 1))
    sent("gather", span(left, 6 * SUB))
    sent("lines", span(left, 24 * SUB))
    landed(gin, oner.at[4])
    inverse = inverse_factor(gsum[...] + gin[...], ({}, {3: add_across}))
    landed(span(zall, (OWNERS - 1) * PIECE), oner.at[7])
    w1 = inverse.astype(BF16)
    w2 = (inverse - w1.astype(F32)).astype(BF16)

    def apply(matrix, dim):
        dims = (((dim,), (0,)), ((), ()))
        return sum(lax.dot_general(w, matrix, dims, preferred_element_type=F32) for w in (w1, w2))

    factor = (apply(zall[...], 1) / PODS).astype(BF16)
    new_factor[...] = factor.T
    mix = apply(factor, 0)
    head = mix.astype(BF16)
    mixed[:RANK, :] = head
    mixed[RANK:, :] = (mix - head.astype(F32)).astype(BF16)

    landed(span(left, MINE), oner.at[3])
    load_momentum.wait()
    sent("cross", span(left, MINE))
    sent("gram", gsum)
    sent("right", span(zr, OWNERS - 1))
    sent("across", zown)
    sent("back", span(zr, OWNERS - 1))


def gather(delta, error, momentum, q):
    vmem, hbm = (pl.BlockSpec(memory_space=s) for s in (pltpu.VMEM, pltpu.HBM))
    dma = pltpu.SemaphoreType.DMA
    wide, square = (ROWS, RANK), (RANK, RANK)
    return pl.pallas_call(
        exchange,
        out_shape=(
            jax.ShapeDtypeStruct(wide, BF16),
            jax.ShapeDtypeStruct(wide, BF16),
            jax.ShapeDtypeStruct(wide, BF16),
            jax.ShapeDtypeStruct((2 * RANK, RANK), BF16),
            jax.ShapeDtypeStruct(square, BF16),
        ),
        in_specs=[hbm] * 4,
        out_specs=(vmem,) * 5,
        scratch_shapes=[
            pltpu.VMEM(square, BF16),
            pltpu.VMEM(wide, BF16),
            pltpu.VMEM(wide, BF16),
            pltpu.VMEM((MINE, RANK), BF16),
            pltpu.VMEM((MINE, RANK), BF16),
            pltpu.VMEM((NY, NX, SUB, RANK), BF16),
            pltpu.VMEM((NX, NY, SUB, RANK), BF16),
            pltpu.VMEM((2, LINE, RANK), BF16),
            pltpu.VMEM((2, NX, LINE, RANK), BF16),
            pltpu.VMEM((2, LINE, RANK), F32),
            pltpu.VMEM((2, SUB, RANK), F32),
            pltpu.VMEM((2, LINE, RANK), BF16),
            pltpu.VMEM((2, NY, SUB, RANK), BF16),
            pltpu.VMEM((2, 2, SUB, HALF), BF16),
            pltpu.VMEM((NZ, 2, TILE, HALF), BF16),
            pltpu.VMEM((2, 2, SUB, HALF), F32),
            pltpu.VMEM((NZ, 2, TILE, HALF), BF16),
            pltpu.VMEM((2 * NX,) + square, F32),
            pltpu.VMEM(square, F32),
            pltpu.VMEM(square, F32),
            pltpu.VMEM(square, F32),
            pltpu.VMEM(square, BF16),
            pltpu.VMEM((OWNERS, PIECE, RANK), BF16),
            pltpu.VMEM((PIECE, RANK), BF16),
            pltpu.VMEM((PIECE, RANK), BF16),
            pltpu.VMEM(square, BF16),
            dma((10,)), dma((13,)), dma((NX,)), dma((2,)), dma((2,)), dma((8,)), dma((2, NY)), dma((2, NX, NY)),
        ],
        compiler_params=pltpu.CompilerParams(collective_id=0, has_side_effects=True, vmem_limit_bytes=32 << 20),
        cost_estimate=pl.CostEstimate(flops=6 * ROWS * RANK * RANK, bytes_accessed=5 * ROWS * RANK * 2, transcendentals=0),
        name="gather_left",
    )(*(pltpu.with_memory_space_constraint(a, pltpu.HBM) for a in (delta, error, momentum, q)))


def finish(left, merged, momentum, mixed, factor, new_error, new_momentum, outer_step, new_factor, e, m, s, sem):
    size, count = ROWS // 8, 8
    copies = [pltpu.make_async_copy(factor, new_factor, sem.at[count, 0])]
    copies[0].start()
    for i in range(count):
        at = pl.ds(i * size, size)
        block = left[at, :]
        approx = jnp.dot(jnp.concatenate([block, block], axis=1), mixed[...], preferred_element_type=F32)
        e[at, :] = (merged[at, :].astype(F32) - approx).astype(BF16)
        moment = 0.9 * momentum[at, :].astype(F32) + approx
        m[at, :] = moment.astype(BF16)
        s[at, :] = (0.7 * (approx + 0.9 * moment)).astype(BF16)
        for k, (src, dst) in enumerate(((e, new_error.at[0, at]), (m, new_momentum.at[at]), (s, outer_step.at[at]))):
            copies.append(pltpu.make_async_copy(src.at[at], dst, sem.at[i, k]))
            copies[-1].start()
    for copy in copies:
        copy.wait()


def outputs(left, merged, momentum, mixed, factor):
    any_, vmem = pl.BlockSpec(memory_space=pl.ANY), pl.BlockSpec(memory_space=pltpu.VMEM)
    wide = (ROWS, RANK)
    return pl.pallas_call(
        finish,
        out_shape=(
            jax.ShapeDtypeStruct((1,) + wide, BF16),
            jax.ShapeDtypeStruct(wide, BF16),
            jax.ShapeDtypeStruct(wide, BF16),
            jax.ShapeDtypeStruct((RANK, RANK), BF16),
        ),
        in_specs=[vmem] * 5,
        out_specs=(any_,) * 4,
        scratch_shapes=[pltpu.VMEM(wide, BF16)] * 3 + [pltpu.SemaphoreType.DMA((9, 3))],
        compiler_params=pltpu.CompilerParams(vmem_limit_bytes=24 << 20),
        cost_estimate=pl.CostEstimate(flops=4 * ROWS * RANK * RANK, bytes_accessed=6 * ROWS * RANK * 2, transcendentals=0),
        name="outputs",
    )(left, merged, momentum, mixed, factor)


def body(delta, error, momentum, q_init):
    left, merged, held, mixed, factor = gather(delta, error, momentum, q_init)
    return outputs(left, merged, held, mixed, factor)


def solution(mesh):
    placed = (P("outer", None, "tp"), P("outer", None, "tp"), P(None, "tp"), P("tp", None))
    return jax.shard_map(
        body,
        mesh=mesh,
        in_specs=placed,
        out_specs=(P("outer", None, "tp"), P(None, "tp"), P(None, "tp"), P("tp", None)),
        check_vma=False,
    )
```

```python
import jax
import jax.numpy as jnp
from jax import lax
from jax.experimental import pallas as pl
from jax.experimental.pallas import tpu as pltpu
from jax.sharding import PartitionSpec as P

MESH = pl.DeviceIdType.MESH
F32, BF16 = jnp.float32, jnp.bfloat16
NX, NY, NZ, ZLO = 4, 4, 8, 4
ROWS, RANK, HALF = 4096, 256, 128
MINE = ROWS // 2
PART = MINE // 2
LINE = PART // NX
SUB = LINE // NY
TILE = 16
PODS = 16
OWNERS = 2 * NX
PIECE = RANK // OWNERS


HIGH = lax.Precision.HIGHEST


def mm(a, b, dims):
    return lax.dot_general(a, b, (dims, ((), ())), precision=HIGH, preferred_element_type=F32)


def reciprocal(d):
    return pltpu.reciprocal(d, approx=True)


def factor_block(a):
    tile = (8, 128)
    lane = lax.broadcasted_iota(jnp.int32, tile, 1)
    row = lax.broadcasted_iota(jnp.int32, tile, 0)

    def turn(k, tiles):
        finished = lane >= 128 - 32 * k
        pivots, following, rest = tiles[0], tiles[1], tiles[2:]
        done = []
        for g in range(4):
            first = 8 * g
            here = (lane >= first) & (lane < first + 8)

            def column(x, c):
                return jnp.broadcast_to(x[:, first + c:first + c + 1], tile)

            def line(x, r):
                return jnp.broadcast_to(x[r:r + 1], tile)

            lefts = [column(pivots, c) for c in range(8)]
            block = {(r, c): line(lefts[c], r) for c in range(8) for r in range(c, 8)}
            own = jnp.where(here, jnp.where(lane - first == row, 1.0, 0.0), pivots)
            lines = [line(own, r) for r in range(8)]
            below = [column(following, c) for c in range(8)]
            following = jnp.where(here, 0.0, following)
            diag = jnp.ones(tile, F32)
            upper = own
            for p in range(0, 8, 2):
                q = p + 1
                d_p, d_pq, d_q = block[p, p], block[q, p], block[q, q]
                det = d_p * d_q - d_pq * d_pq
                inv_p = reciprocal(d_p)
                inv_q = d_p * reciprocal(det)
                ratio = d_pq * inv_p
                lines[q] = lines[q] - ratio * lines[p]
                diag = jnp.where(row == p, d_p, jnp.where(row == q, det * inv_p, diag))
                upper = jnp.where(row == q, lines[q], upper)
                later = range(q + 1, 8)
                edge_p = {k: block[k, p] for k in later}
                edge_q = {k: block[k, q] - ratio * edge_p[k] for k in later}
                part_p = {k: edge_p[k] * inv_p for k in later}
                part_q = {k: edge_q[k] * inv_q for k in later}
                for c in later:
                    for r in range(c, 8):
                        block[r, c] = block[r, c] - part_p[r] * edge_p[c] - part_q[r] * edge_q[c]
                for k in later:
                    lines[k] = lines[k] - part_p[k] * lines[p] - part_q[k] * lines[q]
                if p < 6:
                    upper = jnp.where(row == q + 1, lines[q + 1], upper)
                below_p = below[p] * inv_p
                below_q = (below[q] - below_p * d_pq) * inv_q
                following = following - below_p * lines[p] - below_q * lines[q]
                for k in later:
                    below[k] = below[k] - below_p * edge_p[k] - below_q * edge_q[k]
            done.append(jnp.where((lane <= row + first) | finished, upper * (1.0 / jnp.sqrt(diag)), 0.0))
            factors = jnp.where(finished, 0.0, upper / diag).T[first + 16:].reshape(rest.shape[0], 8, 8)
            rest = jnp.where(here, 0.0, rest)
            for c in range(8):
                rest = rest - factors[:, :, c:c + 1] * lines[c]
            if g < 3:
                pivots, following, rest = following, rest[0], rest[1:]
        tiles = [following] + [rest[t] for t in range(11)] + done
        return jnp.stack([pltpu.roll(x, 96, 1) for x in tiles])

    return lax.fori_loop(0, 4, turn, a.reshape(16, 8, 128)).reshape(128, 128)


def inverse_factor(gram, between):
    on = lax.broadcasted_iota(jnp.int32, gram.shape, 0) == lax.broadcasted_iota(jnp.int32, gram.shape, 1)
    diagonal = jnp.where(on, gram, 0.0)
    scale = 1.0 / jnp.sqrt(jnp.sum(diagonal, axis=0, keepdims=True))
    gram = gram * scale * (1.0 / jnp.sqrt(jnp.sum(diagonal, axis=1, keepdims=True)))
    w11 = factor_block(gram[:128, :128])
    between()
    l21 = mm(gram[128:, :128], w11, ((1,), (1,)))
    corner = mm(l21, w11, ((1,), (0,)))
    w22 = factor_block(gram[128:, 128:] - mm(l21, l21, ((1,), (1,))))
    w21 = -mm(w22, corner, ((1,), (0,)))
    top = jnp.concatenate([w11, jnp.zeros((128, 128), F32)], axis=1)
    return jnp.concatenate([top, jnp.concatenate([w21, w22], axis=1)], axis=0) * scale


def device(x, y, z, core):
    return ((z // ZLO) * NX + x) * 2 + core, (z % ZLO) * NY + y


def send(src, dst, send_sem, recv_sem, dev):
    return pltpu.make_async_remote_copy(
        src_ref=src, dst_ref=dst, send_sem=send_sem, recv_sem=recv_sem, device_id=dev, device_id_type=MESH
    )


def exchange(
    delta, error, momentum, q_in, left, merged, held, mixed, new_factor,
    q, dbuf, ebuf, pair_in, s1, xs, rx, sx, r1, o1, o2, s2, r2, s3, r3, o3, g3,
    gpart, gsum, gin, zsum, zsend, zr, zown, zpair, zall,
    ld, ss, cr, p1r, p2r, oner, a2r, a1r,
):
    o, t = lax.axis_index("outer"), lax.axis_index("tp")
    core, x, y = lax.rem(o, 2), lax.rem(o // 2, NX), lax.rem(t, NY)
    z = (o // (2 * NX)) * ZLO + t // NY
    sibling = device(x, y, z, 1 - core)
    c1, c2 = (x, y), (y, x)

    def peer1(h, v):
        return device(v, y, z, core) if h == 0 else device(x, v, z, core)

    def peer2(h, v):
        return device(x, v, z, core) if h == 0 else device(v, y, z, core)

    def turn(v, i, n):
        return lax.rem(v + i, n)

    def rows(start, size):
        return pl.ds(pl.multiple_of(start, TILE), size)

    mine, theirs = core * MINE, (1 - core) * MINE

    def line(h, i):
        return h * PART + turn(c1[h], i, NX) * LINE

    order = [(whose, i) for whose in range(2) for i in (2, 3, 1, 0)]

    def loads(whose, i, h):
        src, k = rows((mine if whose else theirs) + line(h, i), LINE), whose * NX + i
        return (
            pltpu.make_async_copy(delta.at[0, src], dbuf.at[src], ld.at[k]),
            pltpu.make_async_copy(error.at[0, src], ebuf.at[src], ld.at[k]),
        )

    def fetch(part):
        for whose, i in part:
            for h in range(2):
                for copy in loads(whose, i, h):
                    copy.start()

    fetch(order[:2])
    barrier = pltpu.get_barrier_semaphore()
    greeted = [sibling]
    greeted += [device(turn(x, i, NX), y, z, core) for i in range(1, NX)]
    greeted += [device(x, turn(y, i, NY), z, core) for i in range(1, NY)]
    greeted += [device(x, y, turn(z, i, NZ), core) for i in range(1, NZ)]
    greeted += [device(turn(x, i, NX), y, z, 1 - core) for i in range(1, NX)]
    for dev in greeted:
        pl.semaphore_signal(barrier, inc=1, device_id=dev, device_id_type=MESH)

    fetch(order[2:])
    load_q = pltpu.make_async_copy(q_in, q, ld.at[8])
    load_q.start()

    stages = ("core", "first", "second", "z", "merged", "tiles", "gather", "lines", "cross", "gram", "right", "across", "back")

    def go(stage, src, dst, recv_sem, dev):
        send(src, dst, ss.at[stages.index(stage)], recv_sem, dev).start()

    def sent(stage, ref):
        sem = ss.at[stages.index(stage)]
        send(ref, ref, sem, sem, sibling).wait_send()

    def landed(ref, sem):
        send(ref, ref, ss.at[0], sem, sibling).wait_recv()

    def span(ref, size):
        return ref.at[pl.ds(0, size)]

    def merge(whose, i, h):
        if h == 0:
            every = span(dbuf, 4 * LINE)
            pltpu.make_async_copy(every, every, ld.at[whose * NX + i]).wait()
        block = rows((mine if whose else theirs) + line(h, i), LINE)
        total = (dbuf[block, :].astype(F32) + ebuf[block, :].astype(F32)).astype(BF16)
        merged[block, :] = total
        return block, total.astype(F32)

    def give(i, h):
        block, _ = merge(0, i, h)
        here = rows(line(h, i), LINE)
        go("core", merged.at[block], pair_in.at[here], cr.at[i], sibling)

    def take(i, h):
        _, total = merge(1, i, h)
        at = line(h, i)
        here = rows(at, LINE)
        if h == 0:
            landed(span(pair_in, 2 * LINE), cr.at[i])
        total = total + pair_in[here, :].astype(F32)
        if h == 1:
            both = total.astype(BF16)
            xs[turn(y, i, NY)] = both.reshape(NX, SUB, RANK)
            total = jnp.dot(both, q[...], preferred_element_type=F32)
        if not isinstance(i, int):
            s1[here, :] = total.astype(BF16)
            go("first", s1.at[here], r1.at[h, c1[h]], p1r.at[h], peer1(h, turn(c1[h], i, NX)))
        else:
            o1[h] = total

    pl.semaphore_wait(barrier, len(greeted))
    for step in (give, take):
        if step is take:
            load_q.wait()

        @pl.loop(0, NX - 1)
        def _(n, step=step):
            for h in range(2):
                step(1 + lax.rem(n + 1, NX - 1), h)

        for h in range(2):
            step(0, h)

    load_momentum = pltpu.make_async_copy(momentum, held, ld.at[9])
    load_momentum.start()

    for h in range(2):
        landed(span(s1, 3 * LINE), p1r.at[h])
        for i in (2, 1, 3, 0):
            b = turn(c2[h], i, NY)
            at = rows(b * SUB, SUB)
            total = o1[h, at, :]
            for j in range(1, NX):
                total += r1[h, turn(c1[h], j, NX), at, :].astype(F32)
            if h == 0:
                both = total.astype(BF16)
                sx[0, at, :] = both
                total = jnp.dot(both, q[...], preferred_element_type=F32)
            if i:
                s2[h, at, :] = total.astype(BF16)
                go("second", s2.at[h, at], r2.at[h, c2[h]], p2r.at[h], peer2(h, b))
            else:
                o2[h] = total
    for h in range(2):
        landed(r2.at[h, pl.ds(0, NY - 1)], p2r.at[h])
        total = o2[h]
        for i in range(1, NY):
            total += r2[h, turn(c2[h], i, NY)].astype(F32)
        for c in range(2):
            o3[h, c] = total[:, c * HALF:(c + 1) * HALF]
            s3[h, c] = total[:, c * HALF:(c + 1) * HALF].astype(BF16)

    far = (4, 3, 5, 2, 6, 1, 7)

    def spot(v):
        return v // 4, rows((v % 4) * TILE, TILE)

    for i in far:
        b = turn(z, i, NZ)
        c, at = spot(b)
        go("z", s3.at[:, c, at], r3.at[z], oner.at[0], device(x, y, b, core))
    for i in (2, 1, 3):
        b = turn(x, i, NX)
        go("merged", xs.at[:, b], rx.at[x], oner.at[1], device(b, y, z, core))
    sent("core", span(left, 2 * PART))
    sent("first", span(left, 6 * LINE))
    sent("second", span(left, 6 * SUB))
    landed(span(r3, NZ - 1), oner.at[0])

    def sub(h, i, j):
        return rows(mine + line(h, i) + turn(c2[h], j, NY) * SUB, SUB)

    c, at = spot(z)
    for h in range(2):
        total = o3[h, c, at, :]
        for i in range(1, NZ):
            total += r3[turn(z, i, NZ), h].astype(F32)
        g3[z, h] = total.astype(BF16)
    for i in far:
        b = turn(z, i, NZ)
        go("tiles", g3.at[z], g3.at[z], oner.at[2], device(x, y, b, core))

    def along(h, j):
        at, b = left.at[sub(h, 0, j)], turn(c2[h], j, NY)
        for i in (2, 1, 3):
            go("lines", at, at, a1r.at[h, c1[h], b], peer1(h, turn(c1[h], i, NX)))

    def arrive(h, i, j):
        landed(left.at[sub(h, i, j)], a1r.at[h, turn(c1[h], i, NX), turn(c2[h], j, NY)])

    def cross(h, i):
        at = left.at[rows(mine + line(h, i), LINE)]
        go("cross", at, at, oner.at[3], sibling)

    def across_rows(a, b):
        return lax.dot_general(a, b, (((0,), (0,)), ((), ())), preferred_element_type=F32)

    def products(h, i):
        part = left[rows(mine + line(h, i), LINE), :]
        gpart[h * NX + turn(c1[h], i, NX)] = across_rows(part, part)

    landed(span(g3, NZ - 1), oner.at[2])
    for h in range(2):
        left[sub(h, 0, 0), :] = jnp.concatenate(
            [jnp.concatenate([g3[c * 4 + v, h] for c in range(2)], axis=1) for v in range(4)], axis=0
        )
        at = left.at[sub(h, 0, 0)]
        for i in (2, 1, 3):
            b = turn(c2[h], i, NY)
            go("gather", at, at, a2r.at[h, c2[h]], peer2(h, b))
        along(h, 0)
    landed(span(rx, NX - 1), oner.at[1])
    owned = xs[:, x].astype(F32)
    for i in range(1, NX):
        owned += rx[turn(x, i, NX)].astype(F32)
    sx[1] = owned.astype(BF16).reshape(LINE, RANK)
    for j in (1, 3, 2):
        for h in range(2):
            at, b = left.at[sub(h, 0, j)], turn(c2[h], j, NY)
            landed(at, a2r.at[h, b])
            along(h, j)
    for h in range(2):
        cross(h, 0)

    owner = x * 2 + core
    others = [(turn(x, i, NX), lax.rem(core + e, 2)) for i in range(NX) for e in range(2) if i or e]

    def piece(v, c):
        return rows((v * 2 + c) * PIECE, PIECE)

    total = across_rows(left[rows(mine + line(0, 0), LINE), :], sx[0])
    for i in (1, 3, 2):
        arrive(1, i, 0)
    owned = jnp.concatenate([left[rows(mine + PART + v * LINE + x * SUB, SUB), :] for v in range(NY)], axis=0)
    zsum[...] = total + across_rows(owned, sx[1])
    zsend[...] = zsum[...].astype(BF16)
    for v, c in others:
        go("right", zsend.at[piece(v, c)], zr.at[owner], oner.at[5], device(v, y, z, c))

    for h in range(2):
        products(h, 0)
    for i in (1, 3, 2):
        for h in range(2):
            for j in (0, 1, 3, 2)[h:]:
                arrive(h, i, j)
            if i != 2:
                cross(h, i)
            products(h, i)

    total = gpart[0]
    for i in range(1, 2 * NX):
        total += gpart[i]
    gsum[...] = total
    go("gram", gsum, gin, oner.at[4], sibling)

    for h in range(2):
        cross(h, 2)
    across = device(x, y, turn(z, ZLO, NZ), core)

    def add_pieces():
        landed(span(zr, OWNERS - 1), oner.at[5])
        total = zsum[piece(x, core), :]
        for v, c in others:
            total += zr[v * 2 + c].astype(F32)
        zown[...] = total.astype(BF16)
        go("across", zown, zpair, oner.at[6], across)

    def add_across():
        landed(zpair, oner.at[6])
        here = piece(x, core)
        zall[here, :] = (zown[...].astype(F32) + zpair[...].astype(F32)).astype(BF16)
        for v, c in others:
            go("back", zall.at[here], zall.at[here], oner.at[7], device(v, y, z, c))

    add_pieces()
    sent("z", span(r3, NZ - 1))
    sent("merged", span(rx, NX - 1))
    sent("tiles", span(r3, NZ - 1))
    sent("gather", span(left, 6 * SUB))
    sent("lines", span(left, 24 * SUB))
    landed(gin, oner.at[4])
    inverse = inverse_factor(gsum[...] + gin[...], add_across)
    landed(span(zall, (OWNERS - 1) * PIECE), oner.at[7])
    w1 = inverse.astype(BF16)
    w2 = (inverse - w1.astype(F32)).astype(BF16)

    def apply(matrix, dim):
        dims = (((dim,), (0,)), ((), ()))
        return sum(lax.dot_general(w, matrix, dims, preferred_element_type=F32) for w in (w1, w2))

    factor = (apply(zall[...], 1) / PODS).astype(BF16)
    new_factor[...] = factor.T
    mix = apply(factor, 0)
    head = mix.astype(BF16)
    mixed[:RANK, :] = head
    mixed[RANK:, :] = (mix - head.astype(F32)).astype(BF16)

    landed(span(left, MINE), oner.at[3])
    load_momentum.wait()
    sent("cross", span(left, MINE))
    sent("gram", gsum)
    sent("right", span(zr, OWNERS - 1))
    sent("across", zown)
    sent("back", span(zr, OWNERS - 1))


def gather(delta, error, momentum, q):
    vmem, hbm = (pl.BlockSpec(memory_space=s) for s in (pltpu.VMEM, pltpu.HBM))
    dma = pltpu.SemaphoreType.DMA
    wide, square = (ROWS, RANK), (RANK, RANK)
    return pl.pallas_call(
        exchange,
        out_shape=(
            jax.ShapeDtypeStruct(wide, BF16),
            jax.ShapeDtypeStruct(wide, BF16),
            jax.ShapeDtypeStruct(wide, BF16),
            jax.ShapeDtypeStruct((2 * RANK, RANK), BF16),
            jax.ShapeDtypeStruct(square, BF16),
        ),
        in_specs=[hbm] * 4,
        out_specs=(vmem,) * 5,
        scratch_shapes=[
            pltpu.VMEM(square, BF16),
            pltpu.VMEM(wide, BF16),
            pltpu.VMEM(wide, BF16),
            pltpu.VMEM((MINE, RANK), BF16),
            pltpu.VMEM((MINE, RANK), BF16),
            pltpu.VMEM((NY, NX, SUB, RANK), BF16),
            pltpu.VMEM((NX, NY, SUB, RANK), BF16),
            pltpu.VMEM((2, LINE, RANK), BF16),
            pltpu.VMEM((2, NX, LINE, RANK), BF16),
            pltpu.VMEM((2, LINE, RANK), F32),
            pltpu.VMEM((2, SUB, RANK), F32),
            pltpu.VMEM((2, LINE, RANK), BF16),
            pltpu.VMEM((2, NY, SUB, RANK), BF16),
            pltpu.VMEM((2, 2, SUB, HALF), BF16),
            pltpu.VMEM((NZ, 2, TILE, HALF), BF16),
            pltpu.VMEM((2, 2, SUB, HALF), F32),
            pltpu.VMEM((NZ, 2, TILE, HALF), BF16),
            pltpu.VMEM((2 * NX,) + square, F32),
            pltpu.VMEM(square, F32),
            pltpu.VMEM(square, F32),
            pltpu.VMEM(square, F32),
            pltpu.VMEM(square, BF16),
            pltpu.VMEM((OWNERS, PIECE, RANK), BF16),
            pltpu.VMEM((PIECE, RANK), BF16),
            pltpu.VMEM((PIECE, RANK), BF16),
            pltpu.VMEM(square, BF16),
            dma((10,)), dma((13,)), dma((NX,)), dma((2,)), dma((2,)), dma((8,)), dma((2, NY)), dma((2, NX, NY)),
        ],
        compiler_params=pltpu.CompilerParams(collective_id=0, has_side_effects=True, vmem_limit_bytes=32 << 20),
        cost_estimate=pl.CostEstimate(flops=6 * ROWS * RANK * RANK, bytes_accessed=5 * ROWS * RANK * 2, transcendentals=0),
        name="gather_left",
    )(*(pltpu.with_memory_space_constraint(a, pltpu.HBM) for a in (delta, error, momentum, q)))


def finish(left, merged, momentum, mixed, factor, new_error, new_momentum, outer_step, new_factor, e, m, s, sem):
    size, count = ROWS // 8, 8
    copies = [pltpu.make_async_copy(factor, new_factor, sem.at[count, 0])]
    copies[0].start()
    for i in range(count):
        at = pl.ds(i * size, size)
        block = left[at, :]
        approx = jnp.dot(jnp.concatenate([block, block], axis=1), mixed[...], preferred_element_type=F32)
        e[at, :] = (merged[at, :].astype(F32) - approx).astype(BF16)
        moment = 0.9 * momentum[at, :].astype(F32) + approx
        m[at, :] = moment.astype(BF16)
        s[at, :] = (0.7 * (approx + 0.9 * moment)).astype(BF16)
        for k, (src, dst) in enumerate(((e, new_error.at[0, at]), (m, new_momentum.at[at]), (s, outer_step.at[at]))):
            copies.append(pltpu.make_async_copy(src.at[at], dst, sem.at[i, k]))
            copies[-1].start()
    for copy in copies:
        copy.wait()


def outputs(left, merged, momentum, mixed, factor):
    any_, vmem = pl.BlockSpec(memory_space=pl.ANY), pl.BlockSpec(memory_space=pltpu.VMEM)
    wide = (ROWS, RANK)
    return pl.pallas_call(
        finish,
        out_shape=(
            jax.ShapeDtypeStruct((1,) + wide, BF16),
            jax.ShapeDtypeStruct(wide, BF16),
            jax.ShapeDtypeStruct(wide, BF16),
            jax.ShapeDtypeStruct((RANK, RANK), BF16),
        ),
        in_specs=[vmem] * 5,
        out_specs=(any_,) * 4,
        scratch_shapes=[pltpu.VMEM(wide, BF16)] * 3 + [pltpu.SemaphoreType.DMA((9, 3))],
        compiler_params=pltpu.CompilerParams(vmem_limit_bytes=24 << 20),
        cost_estimate=pl.CostEstimate(flops=4 * ROWS * RANK * RANK, bytes_accessed=6 * ROWS * RANK * 2, transcendentals=0),
        name="outputs",
    )(left, merged, momentum, mixed, factor)


def body(delta, error, momentum, q_init):
    left, merged, held, mixed, factor = gather(delta, error, momentum, q_init)
    return outputs(left, merged, held, mixed, factor)


def solution(mesh):
    placed = (P("outer", None, "tp"), P("outer", None, "tp"), P(None, "tp"), P("tp", None))
    return jax.shard_map(
        body,
        mesh=mesh,
        in_specs=placed,
        out_specs=(P("outer", None, "tp"), P(None, "tp"), P(None, "tp"), P("tp", None)),
        check_vma=False,
    )
```

```python
import jax
import jax.numpy as jnp
from jax import lax
from jax.experimental import pallas as pl
from jax.experimental.pallas import tpu as pltpu
from jax.sharding import PartitionSpec as P

MESH = pl.DeviceIdType.MESH
F32, BF16 = jnp.float32, jnp.bfloat16
NX, NY, NZ, ZLO = 4, 4, 8, 4
ROWS, RANK, HALF = 4096, 256, 128
MINE = ROWS // 2
PART = MINE // 2
LINE = PART // NX
SUB = LINE // NY
TILE = 16
PODS = 16
OWNERS = 2 * NX
PIECE = RANK // OWNERS


HIGH = lax.Precision.HIGHEST


def mm(a, b, dims):
    return lax.dot_general(a, b, (dims, ((), ())), precision=HIGH, preferred_element_type=F32)


def reciprocal(d):
    return pltpu.reciprocal(d, approx=True)


def factor_block(a):
    tile = (8, 128)
    lane = lax.broadcasted_iota(jnp.int32, tile, 1)
    row = lax.broadcasted_iota(jnp.int32, tile, 0)

    def turn(k, tiles):
        finished = lane >= 128 - 32 * k
        pivots, following, rest = tiles[0], tiles[1], tiles[2:]
        done = []
        for g in range(4):
            first = 8 * g
            here = (lane >= first) & (lane < first + 8)

            def column(x, c):
                return jnp.broadcast_to(x[:, first + c:first + c + 1], tile)

            def line(x, r):
                return jnp.broadcast_to(x[r:r + 1], tile)

            lefts = [column(pivots, c) for c in range(8)]
            block = {(r, c): line(lefts[c], r) for c in range(8) for r in range(c, 8)}
            own = jnp.where(here, jnp.where(lane - first == row, 1.0, 0.0), pivots)
            lines = [line(own, r) for r in range(8)]
            below = [column(following, c) for c in range(8)]
            following = jnp.where(here, 0.0, following)
            diag = jnp.ones(tile, F32)
            upper = own
            for p in range(0, 8, 2):
                q = p + 1
                d_p, d_pq, d_q = block[p, p], block[q, p], block[q, q]
                det = d_p * d_q - d_pq * d_pq
                inv_p = reciprocal(d_p)
                inv_q = d_p * reciprocal(det)
                ratio = d_pq * inv_p
                lines[q] = lines[q] - ratio * lines[p]
                diag = jnp.where(row == p, d_p, jnp.where(row == q, det * inv_p, diag))
                upper = jnp.where(row == q, lines[q], upper)
                later = range(q + 1, 8)
                edge_p = {k: block[k, p] for k in later}
                edge_q = {k: block[k, q] - ratio * edge_p[k] for k in later}
                part_p = {k: edge_p[k] * inv_p for k in later}
                part_q = {k: edge_q[k] * inv_q for k in later}
                for c in later:
                    for r in range(c, 8):
                        block[r, c] = block[r, c] - part_p[r] * edge_p[c] - part_q[r] * edge_q[c]
                for k in later:
                    lines[k] = lines[k] - part_p[k] * lines[p] - part_q[k] * lines[q]
                if p < 6:
                    upper = jnp.where(row == q + 1, lines[q + 1], upper)
                below_p = below[p] * inv_p
                below_q = (below[q] - below_p * d_pq) * inv_q
                following = following - below_p * lines[p] - below_q * lines[q]
                for k in later:
                    below[k] = below[k] - below_p * edge_p[k] - below_q * edge_q[k]
            done.append(jnp.where((lane <= row + first) | finished, upper * (1.0 / jnp.sqrt(diag)), 0.0))
            factors = jnp.where(finished, 0.0, upper / diag).T[first + 16:].reshape(rest.shape[0], 8, 8)
            rest = jnp.where(here, 0.0, rest)
            for c in range(8):
                rest = rest - factors[:, :, c:c + 1] * lines[c]
            if g < 3:
                pivots, following, rest = following, rest[0], rest[1:]
        tiles = [following] + [rest[t] for t in range(11)] + done
        return jnp.stack([pltpu.roll(x, 96, 1) for x in tiles])

    return lax.fori_loop(0, 4, turn, a.reshape(16, 8, 128)).reshape(128, 128)


def inverse_factor(gram, between):
    on = lax.broadcasted_iota(jnp.int32, gram.shape, 0) == lax.broadcasted_iota(jnp.int32, gram.shape, 1)
    diagonal = jnp.where(on, gram, 0.0)
    scale = 1.0 / jnp.sqrt(jnp.sum(diagonal, axis=0, keepdims=True))
    gram = gram * scale * (1.0 / jnp.sqrt(jnp.sum(diagonal, axis=1, keepdims=True)))
    w11 = factor_block(gram[:128, :128])
    between()
    l21 = mm(gram[128:, :128], w11, ((1,), (1,)))
    corner = mm(l21, w11, ((1,), (0,)))
    w22 = factor_block(gram[128:, 128:] - mm(l21, l21, ((1,), (1,))))
    w21 = -mm(w22, corner, ((1,), (0,)))
    top = jnp.concatenate([w11, jnp.zeros((128, 128), F32)], axis=1)
    return jnp.concatenate([top, jnp.concatenate([w21, w22], axis=1)], axis=0) * scale


def device(x, y, z, core):
    return ((z // ZLO) * NX + x) * 2 + core, (z % ZLO) * NY + y


def send(src, dst, send_sem, recv_sem, dev):
    return pltpu.make_async_remote_copy(
        src_ref=src, dst_ref=dst, send_sem=send_sem, recv_sem=recv_sem, device_id=dev, device_id_type=MESH
    )


def exchange(
    delta, error, momentum, q_in, left, merged, held, mixed, new_factor,
    q, dbuf, ebuf, pair_in, s1, xs, rx, sx, r1, o1, o2, s2, r2, s3, r3, o3, g3,
    gpart, gsum, gin, zsum, zsend, zr, zown, zpair, zall,
    ld, ss, cr, p1r, p2r, oner, a2r, a1r,
):
    o, t = lax.axis_index("outer"), lax.axis_index("tp")
    core, x, y = lax.rem(o, 2), lax.rem(o // 2, NX), lax.rem(t, NY)
    z = (o // (2 * NX)) * ZLO + t // NY
    sibling = device(x, y, z, 1 - core)
    c1, c2 = (x, y), (y, x)

    def peer1(h, v):
        return device(v, y, z, core) if h == 0 else device(x, v, z, core)

    def peer2(h, v):
        return device(x, v, z, core) if h == 0 else device(v, y, z, core)

    def turn(v, i, n):
        return lax.rem(v + i, n)

    def rows(start, size):
        return pl.ds(pl.multiple_of(start, TILE), size)

    mine, theirs = core * MINE, (1 - core) * MINE

    def line(h, i):
        return h * PART + turn(c1[h], i, NX) * LINE

    order = [(whose, i) for whose in range(2) for i in (2, 1, 3, 0)]

    def loads(whose, i, h):
        src, k = rows((mine if whose else theirs) + line(h, i), LINE), whose * NX + i
        return (
            pltpu.make_async_copy(delta.at[0, src], dbuf.at[src], ld.at[k]),
            pltpu.make_async_copy(error.at[0, src], ebuf.at[src], ld.at[k]),
        )

    def fetch(part):
        for whose, i in part:
            for h in range(2):
                for copy in loads(whose, i, h):
                    copy.start()

    fetch(order[:2])
    barrier = pltpu.get_barrier_semaphore()
    greeted = [sibling]
    greeted += [device(turn(x, i, NX), y, z, core) for i in range(1, NX)]
    greeted += [device(x, turn(y, i, NY), z, core) for i in range(1, NY)]
    greeted += [device(x, y, turn(z, i, NZ), core) for i in range(1, NZ)]
    greeted += [device(turn(x, i, NX), y, z, 1 - core) for i in range(1, NX)]
    for dev in greeted:
        pl.semaphore_signal(barrier, inc=1, device_id=dev, device_id_type=MESH)

    fetch(order[2:])
    load_q = pltpu.make_async_copy(q_in, q, ld.at[8])
    load_q.start()

    stages = ("core", "first", "second", "z", "merged", "tiles", "gather", "lines", "cross", "gram", "right", "across", "back")

    def go(stage, src, dst, recv_sem, dev):
        send(src, dst, ss.at[stages.index(stage)], recv_sem, dev).start()

    def sent(stage, ref):
        sem = ss.at[stages.index(stage)]
        send(ref, ref, sem, sem, sibling).wait_send()

    def landed(ref, sem):
        send(ref, ref, ss.at[0], sem, sibling).wait_recv()

    def span(ref, size):
        return ref.at[pl.ds(0, size)]

    def merge(whose, i, h):
        if h == 0:
            every = span(dbuf, 4 * LINE)
            pltpu.make_async_copy(every, every, ld.at[whose * NX + i]).wait()
        block = rows((mine if whose else theirs) + line(h, i), LINE)
        total = (dbuf[block, :].astype(F32) + ebuf[block, :].astype(F32)).astype(BF16)
        merged[block, :] = total
        return block, total.astype(F32)

    def give(i, h):
        block, _ = merge(0, i, h)
        here = rows(line(h, i), LINE)
        go("core", merged.at[block], pair_in.at[here], cr.at[i], sibling)

    def take(i, h):
        _, total = merge(1, i, h)
        at = line(h, i)
        here = rows(at, LINE)
        if h == 0:
            landed(span(pair_in, 2 * LINE), cr.at[i])
        total = total + pair_in[here, :].astype(F32)
        if h == 1:
            both = total.astype(BF16)
            xs[turn(y, i, NY)] = both.reshape(NX, SUB, RANK)
            total = jnp.dot(both, q[...], preferred_element_type=F32)
        if i:
            s1[here, :] = total.astype(BF16)
            go("first", s1.at[here], r1.at[h, c1[h]], p1r.at[h], peer1(h, turn(c1[h], i, NX)))
        else:
            o1[h] = total

    for n, (whose, i) in enumerate(order):
        if n == 0:
            pl.semaphore_wait(barrier, len(greeted))
        if n == 2:
            load_q.wait()
        for h in range(2):
            if whose:
                take(i, h)
            else:
                give(i, h)

    load_momentum = pltpu.make_async_copy(momentum, held, ld.at[9])
    load_momentum.start()

    for h in range(2):
        landed(span(s1, 3 * LINE), p1r.at[h])
        for i in (2, 1, 3, 0):
            b = turn(c2[h], i, NY)
            at = rows(b * SUB, SUB)
            total = o1[h, at, :]
            for j in range(1, NX):
                total += r1[h, turn(c1[h], j, NX), at, :].astype(F32)
            if h == 0:
                both = total.astype(BF16)
                sx[0, at, :] = both
                total = jnp.dot(both, q[...], preferred_element_type=F32)
            if i:
                s2[h, at, :] = total.astype(BF16)
                go("second", s2.at[h, at], r2.at[h, c2[h]], p2r.at[h], peer2(h, b))
            else:
                o2[h] = total
    for i in (2, 1, 3):
        b = turn(x, i, NX)
        go("merged", xs.at[:, b], rx.at[x], oner.at[1], device(b, y, z, core))
    for h in range(2):
        landed(r2.at[h, pl.ds(0, NY - 1)], p2r.at[h])
        total = o2[h]
        for i in range(1, NY):
            total += r2[h, turn(c2[h], i, NY)].astype(F32)
        for c in range(2):
            o3[h, c] = total[:, c * HALF:(c + 1) * HALF]
            s3[h, c] = total[:, c * HALF:(c + 1) * HALF].astype(BF16)

    far = (4, 3, 5, 2, 6, 1, 7)

    def spot(v):
        return v // 4, rows((v % 4) * TILE, TILE)

    for i in far:
        b = turn(z, i, NZ)
        c, at = spot(b)
        go("z", s3.at[:, c, at], r3.at[z], oner.at[0], device(x, y, b, core))
    sent("core", span(left, 2 * PART))
    sent("first", span(left, 6 * LINE))
    sent("second", span(left, 6 * SUB))
    landed(span(r3, NZ - 1), oner.at[0])

    def sub(h, i, j):
        return rows(mine + line(h, i) + turn(c2[h], j, NY) * SUB, SUB)

    c, at = spot(z)
    for h in range(2):
        total = o3[h, c, at, :]
        for i in range(1, NZ):
            total += r3[turn(z, i, NZ), h].astype(F32)
        g3[z, h] = total.astype(BF16)
    for i in far:
        b = turn(z, i, NZ)
        go("tiles", g3.at[z], g3.at[z], oner.at[2], device(x, y, b, core))

    def along(h, j):
        at, b = left.at[sub(h, 0, j)], turn(c2[h], j, NY)
        for i in (2, 1, 3):
            go("lines", at, at, a1r.at[h, c1[h], b], peer1(h, turn(c1[h], i, NX)))

    def arrive(h, i, j):
        landed(left.at[sub(h, i, j)], a1r.at[h, turn(c1[h], i, NX), turn(c2[h], j, NY)])

    def cross(h, i):
        at = left.at[rows(mine + line(h, i), LINE)]
        go("cross", at, at, oner.at[3], sibling)

    def across_rows(a, b):
        return lax.dot_general(a, b, (((0,), (0,)), ((), ())), preferred_element_type=F32)

    def products(h, i):
        part = left[rows(mine + line(h, i), LINE), :]
        gpart[h * NX + turn(c1[h], i, NX)] = across_rows(part, part)

    landed(span(g3, NZ - 1), oner.at[2])
    for h in range(2):
        left[sub(h, 0, 0), :] = jnp.concatenate(
            [jnp.concatenate([g3[c * 4 + v, h] for c in range(2)], axis=1) for v in range(4)], axis=0
        )
        at = left.at[sub(h, 0, 0)]
        for i in (2, 1, 3):
            b = turn(c2[h], i, NY)
            go("gather", at, at, a2r.at[h, c2[h]], peer2(h, b))
        along(h, 0)
    for j in (1, 3, 2):
        for h in range(2):
            at, b = left.at[sub(h, 0, j)], turn(c2[h], j, NY)
            landed(at, a2r.at[h, b])
            along(h, j)
    for h in range(2):
        cross(h, 0)

    owner = x * 2 + core
    others = [(turn(x, i, NX), lax.rem(core + e, 2)) for i in range(NX) for e in range(2) if i or e]

    def piece(v, c):
        return rows((v * 2 + c) * PIECE, PIECE)

    total = across_rows(left[rows(mine + line(0, 0), LINE), :], sx[0])
    landed(span(rx, NX - 1), oner.at[1])
    owned = xs[:, x].astype(F32)
    for i in range(1, NX):
        owned += rx[turn(x, i, NX)].astype(F32)
    sx[1] = owned.astype(BF16).reshape(LINE, RANK)
    for i in (1, 3, 2):
        arrive(1, i, 0)
    owned = jnp.concatenate([left[rows(mine + PART + v * LINE + x * SUB, SUB), :] for v in range(NY)], axis=0)
    zsum[...] = total + across_rows(owned, sx[1])
    zsend[...] = zsum[...].astype(BF16)
    for v, c in others:
        go("right", zsend.at[piece(v, c)], zr.at[owner], oner.at[5], device(v, y, z, c))

    for h in range(2):
        products(h, 0)
    for i in (1, 3, 2):
        for h in range(2):
            for j in (0, 1, 3, 2)[h:]:
                arrive(h, i, j)
            if i != 2:
                cross(h, i)
            products(h, i)

    total = gpart[0]
    for i in range(1, 2 * NX):
        total += gpart[i]
    gsum[...] = total
    go("gram", gsum, gin, oner.at[4], sibling)

    for h in range(2):
        cross(h, 2)
    across = device(x, y, turn(z, ZLO, NZ), core)

    def add_pieces():
        landed(span(zr, OWNERS - 1), oner.at[5])
        total = zsum[piece(x, core), :]
        for v, c in others:
            total += zr[v * 2 + c].astype(F32)
        zown[...] = total.astype(BF16)
        go("across", zown, zpair, oner.at[6], across)

    def add_across():
        landed(zpair, oner.at[6])
        here = piece(x, core)
        zall[here, :] = (zown[...].astype(F32) + zpair[...].astype(F32)).astype(BF16)
        for v, c in others:
            go("back", zall.at[here], zall.at[here], oner.at[7], device(v, y, z, c))

    add_pieces()
    sent("z", span(r3, NZ - 1))
    sent("merged", span(rx, NX - 1))
    sent("tiles", span(r3, NZ - 1))
    sent("gather", span(left, 6 * SUB))
    sent("lines", span(left, 24 * SUB))
    landed(gin, oner.at[4])
    inverse = inverse_factor(gsum[...] + gin[...], add_across)
    landed(span(zall, (OWNERS - 1) * PIECE), oner.at[7])
    w1 = inverse.astype(BF16)
    w2 = (inverse - w1.astype(F32)).astype(BF16)

    def apply(matrix, dim):
        dims = (((dim,), (0,)), ((), ()))
        return sum(lax.dot_general(w, matrix, dims, preferred_element_type=F32) for w in (w1, w2))

    factor = (apply(zall[...], 1) / PODS).astype(BF16)
    new_factor[...] = factor.T
    mix = apply(factor, 0)
    head = mix.astype(BF16)
    mixed[:RANK, :] = head
    mixed[RANK:, :] = (mix - head.astype(F32)).astype(BF16)

    landed(span(left, MINE), oner.at[3])
    load_momentum.wait()
    sent("cross", span(left, MINE))
    sent("gram", gsum)
    sent("right", span(zr, OWNERS - 1))
    sent("across", zown)
    sent("back", span(zr, OWNERS - 1))


def gather(delta, error, momentum, q):
    vmem, hbm = (pl.BlockSpec(memory_space=s) for s in (pltpu.VMEM, pltpu.HBM))
    dma = pltpu.SemaphoreType.DMA
    wide, square = (ROWS, RANK), (RANK, RANK)
    return pl.pallas_call(
        exchange,
        out_shape=(
            jax.ShapeDtypeStruct(wide, BF16),
            jax.ShapeDtypeStruct(wide, BF16),
            jax.ShapeDtypeStruct(wide, BF16),
            jax.ShapeDtypeStruct((2 * RANK, RANK), BF16),
            jax.ShapeDtypeStruct(square, BF16),
        ),
        in_specs=[hbm] * 4,
        out_specs=(vmem,) * 5,
        scratch_shapes=[
            pltpu.VMEM(square, BF16),
            pltpu.VMEM(wide, BF16),
            pltpu.VMEM(wide, BF16),
            pltpu.VMEM((MINE, RANK), BF16),
            pltpu.VMEM((MINE, RANK), BF16),
            pltpu.VMEM((NY, NX, SUB, RANK), BF16),
            pltpu.VMEM((NX, NY, SUB, RANK), BF16),
            pltpu.VMEM((2, LINE, RANK), BF16),
            pltpu.VMEM((2, NX, LINE, RANK), BF16),
            pltpu.VMEM((2, LINE, RANK), F32),
            pltpu.VMEM((2, SUB, RANK), F32),
            pltpu.VMEM((2, LINE, RANK), BF16),
            pltpu.VMEM((2, NY, SUB, RANK), BF16),
            pltpu.VMEM((2, 2, SUB, HALF), BF16),
            pltpu.VMEM((NZ, 2, TILE, HALF), BF16),
            pltpu.VMEM((2, 2, SUB, HALF), F32),
            pltpu.VMEM((NZ, 2, TILE, HALF), BF16),
            pltpu.VMEM((2 * NX,) + square, F32),
            pltpu.VMEM(square, F32),
            pltpu.VMEM(square, F32),
            pltpu.VMEM(square, F32),
            pltpu.VMEM(square, BF16),
            pltpu.VMEM((OWNERS, PIECE, RANK), BF16),
            pltpu.VMEM((PIECE, RANK), BF16),
            pltpu.VMEM((PIECE, RANK), BF16),
            pltpu.VMEM(square, BF16),
            dma((10,)), dma((13,)), dma((NX,)), dma((2,)), dma((2,)), dma((8,)), dma((2, NY)), dma((2, NX, NY)),
        ],
        compiler_params=pltpu.CompilerParams(collective_id=0, has_side_effects=True, vmem_limit_bytes=32 << 20),
        cost_estimate=pl.CostEstimate(flops=6 * ROWS * RANK * RANK, bytes_accessed=5 * ROWS * RANK * 2, transcendentals=0),
        name="gather_left",
    )(*(pltpu.with_memory_space_constraint(a, pltpu.HBM) for a in (delta, error, momentum, q)))


def finish(left, merged, momentum, mixed, factor, new_error, new_momentum, outer_step, new_factor, e, m, s, sem):
    size, count = ROWS // 8, 8
    copies = [pltpu.make_async_copy(factor, new_factor, sem.at[count, 0])]
    copies[0].start()
    for i in range(count):
        at = pl.ds(i * size, size)
        block = left[at, :]
        approx = jnp.dot(jnp.concatenate([block, block], axis=1), mixed[...], preferred_element_type=F32)
        e[at, :] = (merged[at, :].astype(F32) - approx).astype(BF16)
        moment = 0.9 * momentum[at, :].astype(F32) + approx
        m[at, :] = moment.astype(BF16)
        s[at, :] = (0.7 * (approx + 0.9 * moment)).astype(BF16)
        for k, (src, dst) in enumerate(((e, new_error.at[0, at]), (m, new_momentum.at[at]), (s, outer_step.at[at]))):
            copies.append(pltpu.make_async_copy(src.at[at], dst, sem.at[i, k]))
            copies[-1].start()
    for copy in copies:
        copy.wait()


def outputs(left, merged, momentum, mixed, factor):
    any_, vmem = pl.BlockSpec(memory_space=pl.ANY), pl.BlockSpec(memory_space=pltpu.VMEM)
    wide = (ROWS, RANK)
    return pl.pallas_call(
        finish,
        out_shape=(
            jax.ShapeDtypeStruct((1,) + wide, BF16),
            jax.ShapeDtypeStruct(wide, BF16),
            jax.ShapeDtypeStruct(wide, BF16),
            jax.ShapeDtypeStruct((RANK, RANK), BF16),
        ),
        in_specs=[vmem] * 5,
        out_specs=(any_,) * 4,
        scratch_shapes=[pltpu.VMEM(wide, BF16)] * 3 + [pltpu.SemaphoreType.DMA((9, 3))],
        compiler_params=pltpu.CompilerParams(vmem_limit_bytes=24 << 20),
        cost_estimate=pl.CostEstimate(flops=4 * ROWS * RANK * RANK, bytes_accessed=6 * ROWS * RANK * 2, transcendentals=0),
        name="outputs",
    )(left, merged, momentum, mixed, factor)


def body(delta, error, momentum, q_init):
    left, merged, held, mixed, factor = gather(delta, error, momentum, q_init)
    return outputs(left, merged, held, mixed, factor)


def solution(mesh):
    placed = (P("outer", None, "tp"), P("outer", None, "tp"), P(None, "tp"), P("tp", None))
    return jax.shard_map(
        body,
        mesh=mesh,
        in_specs=placed,
        out_specs=(P("outer", None, "tp"), P(None, "tp"), P(None, "tp"), P("tp", None)),
        check_vma=False,
    )
```

```python
import jax
import jax.numpy as jnp
from jax import lax
from jax.experimental import pallas as pl
from jax.experimental.pallas import tpu as pltpu
from jax.sharding import PartitionSpec as P

MESH = pl.DeviceIdType.MESH
F32, BF16 = jnp.float32, jnp.bfloat16
NX, NY, NZ, ZLO = 4, 4, 8, 4
ROWS, RANK, HALF = 4096, 256, 128
MINE = ROWS // 2
PART = MINE // 2
LINE = PART // NX
SUB = LINE // NY
TILE = 16
PODS = 16
OWNERS = 2 * NX
PIECE = RANK // OWNERS


HIGH = lax.Precision.HIGHEST


def mm(a, b, dims):
    return lax.dot_general(a, b, (dims, ((), ())), precision=HIGH, preferred_element_type=F32)


def reciprocal(d):
    return pltpu.reciprocal(d, approx=True)


def factor_block(a, between):
    tile = (8, 128)
    lane = lax.broadcasted_iota(jnp.int32, tile, 1)
    row = lax.broadcasted_iota(jnp.int32, tile, 0)
    tiles = a.reshape(16, 8, 128)
    both, rest = tiles[:2], tiles[2:]
    done = []
    for g in range(16):
        first = 8 * g
        shape = both.shape
        below = shape[0] - 1
        cols = [jnp.broadcast_to(both[:, :, first + c:first + c + 1], shape) for c in range(8)]
        here = (lane >= first) & (lane < first + 8)
        start = [jnp.where(here, jnp.where(lane - first == row, 1.0, 0.0), both[0])]
        start += [jnp.where(here, 0.0, both[1])] * below
        both = jnp.stack(start)
        diag = jnp.ones(tile, F32)

        def spread(x, r):
            return jnp.broadcast_to(x[0, r:r + 1], tile)

        def after(r, x):
            top = jnp.where(row > r, x[:1], 0.0)
            return jnp.concatenate([top, x[1:]], axis=0) if below else top

        for p in range(0, 8, 2):
            q = p + 1
            d_p, d_pq, d_q = spread(cols[p], p), spread(cols[p], q), spread(cols[q], q)
            det = d_p * d_q - d_pq * d_pq
            inv_p = reciprocal(d_p)
            inv_q = d_p * reciprocal(det)
            ratio = d_pq * inv_p
            line_p = spread(both, p)
            line_q = spread(both, q) - ratio * line_p
            diag = jnp.where(row == p, d_p, jnp.where(row == q, det * inv_p, diag))
            part_p = after(p, cols[p] * inv_p)
            part_q = after(q, (cols[q] - part_p * d_pq) * inv_q)
            both = both - part_p * line_p - part_q * line_q
            for k in range(q + 1, 8):
                edge_p = spread(cols[k], p)
                edge_q = spread(cols[k], q) - ratio * edge_p
                cols[k] = cols[k] - part_p * edge_p - part_q * edge_q
        upper = both[0]
        done.append(jnp.where(lane <= row + first, upper * (1.0 / jnp.sqrt(diag)), 0.0))
        if g < 14:
            factors = (upper / diag).T[first + 16:].reshape(rest.shape[0], 8, 8)
            rest = jnp.where(here, 0.0, rest)
            for c in range(8):
                rest = rest - factors[:, :, c:c + 1] * upper[c:c + 1]
            both = jnp.concatenate([both[1:], rest[:1]], axis=0)
            rest = rest[1:] if g < 13 else None
        elif g < 15:
            both = both[1:]
        if g in between:
            between[g]()
    return jnp.concatenate(done, axis=0)


def inverse_factor(gram, between):
    on = lax.broadcasted_iota(jnp.int32, gram.shape, 0) == lax.broadcasted_iota(jnp.int32, gram.shape, 1)
    diagonal = jnp.where(on, gram, 0.0)
    scale = 1.0 / jnp.sqrt(jnp.sum(diagonal, axis=0, keepdims=True))
    gram = gram * scale * (1.0 / jnp.sqrt(jnp.sum(diagonal, axis=1, keepdims=True)))
    w11 = factor_block(gram[:128, :128], between[0])
    l21 = mm(gram[128:, :128], w11, ((1,), (1,)))
    w22 = factor_block(gram[128:, 128:] - mm(l21, l21, ((1,), (1,))), between[1])
    w21 = -mm(w22, mm(l21, w11, ((1,), (0,))), ((1,), (0,)))
    top = jnp.concatenate([w11, jnp.zeros((128, 128), F32)], axis=1)
    return jnp.concatenate([top, jnp.concatenate([w21, w22], axis=1)], axis=0) * scale


def device(x, y, z, core):
    return ((z // ZLO) * NX + x) * 2 + core, (z % ZLO) * NY + y


def send(src, dst, send_sem, recv_sem, dev):
    return pltpu.make_async_remote_copy(
        src_ref=src, dst_ref=dst, send_sem=send_sem, recv_sem=recv_sem, device_id=dev, device_id_type=MESH
    )


def exchange(
    delta, error, momentum, q_in, left, merged, held, high, low, new_factor,
    q, dbuf, ebuf, pair_in, s1, xs, rx, sx, r1, o1, s2, r2, s3, r3, o3, g3,
    gpart, gsum, gin, zsum, zsend, zr, zown, zpair, zall,
    ld, ss, cr, p1r, p2r, oner, a2r, a1r,
):
    o, t = lax.axis_index("outer"), lax.axis_index("tp")
    core, x, y = lax.rem(o, 2), lax.rem(o // 2, NX), lax.rem(t, NY)
    z = (o // (2 * NX)) * ZLO + t // NY
    sibling = device(x, y, z, 1 - core)
    c1, c2 = (x, y), (y, x)

    def peer1(h, v):
        return device(v, y, z, core) if h == 0 else device(x, v, z, core)

    def peer2(h, v):
        return device(x, v, z, core) if h == 0 else device(v, y, z, core)

    def turn(v, i, n):
        return lax.rem(v + i, n)

    def rows(start, size):
        return pl.ds(pl.multiple_of(start, TILE), size)

    mine, theirs = core * MINE, (1 - core) * MINE

    def line(h, i):
        return h * PART + turn(c1[h], i, NX) * LINE

    order = [(whose, i) for whose in range(2) for i in (2, 1, 3, 0)]

    def loads(whose, i, h):
        src, k = rows((mine if whose else theirs) + line(h, i), LINE), whose * NX + i
        return (
            pltpu.make_async_copy(delta.at[0, src], dbuf.at[src], ld.at[k]),
            pltpu.make_async_copy(error.at[0, src], ebuf.at[src], ld.at[k]),
        )

    barrier = pltpu.get_barrier_semaphore()
    greeted = [sibling]
    greeted += [device(turn(x, i, NX), y, z, core) for i in range(1, NX)]
    greeted += [device(x, turn(y, i, NY), z, core) for i in range(1, NY)]
    greeted += [device(x, y, turn(z, i, NZ), core) for i in range(1, NZ)]
    greeted += [device(turn(x, i, NX), y, z, 1 - core) for i in range(1, NX)]
    for dev in greeted:
        pl.semaphore_signal(barrier, inc=1, device_id=dev, device_id_type=MESH)

    for whose, i in order:
        for h in range(2):
            for copy in loads(whose, i, h):
                copy.start()
    load_q = pltpu.make_async_copy(q_in, q, ld.at[8])
    load_q.start()

    stages = ("core", "first", "second", "z", "merged", "tiles", "gather", "lines", "cross", "gram", "right", "across", "back")

    def go(stage, src, dst, recv_sem, dev):
        send(src, dst, ss.at[stages.index(stage)], recv_sem, dev).start()

    def sent(stage, ref):
        sem = ss.at[stages.index(stage)]
        send(ref, ref, sem, sem, sibling).wait_send()

    def landed(ref, sem):
        send(ref, ref, ss.at[0], sem, sibling).wait_recv()

    def span(ref, size):
        return ref.at[pl.ds(0, size)]

    def merge(whose, i, h):
        if h == 0:
            every = span(dbuf, 4 * LINE)
            pltpu.make_async_copy(every, every, ld.at[whose * NX + i]).wait()
        block = rows((mine if whose else theirs) + line(h, i), LINE)
        total = (dbuf[block, :].astype(F32) + ebuf[block, :].astype(F32)).astype(BF16)
        merged[block, :] = total
        return block, total.astype(F32)

    def give(i, h):
        block, _ = merge(0, i, h)
        here = rows(line(h, i), LINE)
        go("core", merged.at[block], pair_in.at[here], cr.at[i], sibling)

    def take(i, h):
        _, total = merge(1, i, h)
        at = line(h, i)
        here = rows(at, LINE)
        if h == 0:
            landed(span(pair_in, 2 * LINE), cr.at[i])
        total = total + pair_in[here, :].astype(F32)
        if h == 1:
            both = total.astype(BF16)
            xs[turn(y, i, NY)] = both.reshape(NX, SUB, RANK)
            total = jnp.dot(both, q[...], preferred_element_type=F32)
        if i:
            s1[here, :] = total.astype(BF16)
            go("first", s1.at[here], r1.at[h, c1[h]], p1r.at[h], peer1(h, turn(c1[h], i, NX)))
        else:
            o1[h] = total

    for n, (whose, i) in enumerate(order):
        if n == 0:
            pl.semaphore_wait(barrier, len(greeted))
        if n == 2:
            load_q.wait()
        for h in range(2):
            if whose:
                take(i, h)
            else:
                give(i, h)

    load_momentum = pltpu.make_async_copy(momentum, held, ld.at[9])
    load_momentum.start()

    for h in range(2):
        landed(span(s1, 3 * LINE), p1r.at[h])
        total = o1[h]
        for i in range(1, NX):
            total += r1[h, turn(c1[h], i, NX)].astype(F32)
        o1[h] = total
        if h == 0:
            sx[0] = o1[0].astype(BF16)
            o1[0] = jnp.dot(sx[0], q[...], preferred_element_type=F32)
        s2[h] = o1[h].astype(BF16)
        for i in (2, 1, 3):
            b = turn(c2[h], i, NY)
            go("second", s2.at[h, rows(b * SUB, SUB)], r2.at[h, c2[h]], p2r.at[h], peer2(h, b))
    for h in range(2):
        landed(r2.at[h, pl.ds(0, NY - 1)], p2r.at[h])
        total = o1[h, rows(c2[h] * SUB, SUB), :]
        for i in range(1, NY):
            total += r2[h, turn(c2[h], i, NY)].astype(F32)
        for c in range(2):
            o3[h, c] = total[:, c * HALF:(c + 1) * HALF]
            s3[h, c] = total[:, c * HALF:(c + 1) * HALF].astype(BF16)

    far = (4, 3, 5, 2, 6, 1, 7)

    def spot(v):
        return v // 4, rows((v % 4) * TILE, TILE)

    for i in far:
        b = turn(z, i, NZ)
        c, at = spot(b)
        go("z", s3.at[:, c, at], r3.at[z], oner.at[0], device(x, y, b, core))
    for i in (2, 1, 3):
        b = turn(x, i, NX)
        go("merged", xs.at[:, b], rx.at[x], oner.at[1], device(b, y, z, core))
    sent("core", span(left, 2 * PART))
    sent("first", span(left, 6 * LINE))
    sent("second", span(left, 6 * SUB))
    landed(span(r3, NZ - 1), oner.at[0])

    def sub(h, i, j):
        return rows(mine + line(h, i) + turn(c2[h], j, NY) * SUB, SUB)

    c, at = spot(z)
    for h in range(2):
        total = o3[h, c, at, :]
        for i in range(1, NZ):
            total += r3[turn(z, i, NZ), h].astype(F32)
        g3[z, h] = total.astype(BF16)
    for i in far:
        b = turn(z, i, NZ)
        go("tiles", g3.at[z], g3.at[z], oner.at[2], device(x, y, b, core))

    def along(h, j):
        at, b = left.at[sub(h, 0, j)], turn(c2[h], j, NY)
        for i in (2, 1, 3):
            go("lines", at, at, a1r.at[h, c1[h], b], peer1(h, turn(c1[h], i, NX)))

    def arrive(h, i, j):
        landed(left.at[sub(h, i, j)], a1r.at[h, turn(c1[h], i, NX), turn(c2[h], j, NY)])

    def cross(h, i):
        at = left.at[rows(mine + line(h, i), LINE)]
        go("cross", at, at, oner.at[3], sibling)

    def across_rows(a, b):
        return lax.dot_general(a, b, (((0,), (0,)), ((), ())), preferred_element_type=F32)

    def products(h, i):
        part = left[rows(mine + line(h, i), LINE), :]
        gpart[h * NX + turn(c1[h], i, NX)] = across_rows(part, part)

    landed(span(g3, NZ - 1), oner.at[2])
    for h in range(2):
        left[sub(h, 0, 0), :] = jnp.concatenate(
            [jnp.concatenate([g3[c * 4 + v, h] for c in range(2)], axis=1) for v in range(4)], axis=0
        )
        at = left.at[sub(h, 0, 0)]
        for i in (2, 1, 3):
            b = turn(c2[h], i, NY)
            go("gather", at, at, a2r.at[h, c2[h]], peer2(h, b))
        along(h, 0)
    for j in (1, 3, 2):
        for h in range(2):
            at, b = left.at[sub(h, 0, j)], turn(c2[h], j, NY)
            landed(at, a2r.at[h, b])
            along(h, j)
    for h in range(2):
        cross(h, 0)

    owner = x * 2 + core
    others = [(turn(x, i, NX), lax.rem(core + e, 2)) for i in range(NX) for e in range(2) if i or e]

    def piece(v, c):
        return rows((v * 2 + c) * PIECE, PIECE)

    total = across_rows(left[rows(mine + line(0, 0), LINE), :], sx[0])
    landed(span(rx, NX - 1), oner.at[1])
    owned = xs[:, x].astype(F32)
    for i in range(1, NX):
        owned += rx[turn(x, i, NX)].astype(F32)
    sx[1] = owned.astype(BF16).reshape(LINE, RANK)
    for i in (1, 3, 2):
        arrive(1, i, 0)
    owned = jnp.concatenate([left[rows(mine + PART + v * LINE + x * SUB, SUB), :] for v in range(NY)], axis=0)
    zsum[...] = total + across_rows(owned, sx[1])
    zsend[...] = zsum[...].astype(BF16)
    for v, c in others:
        go("right", zsend.at[piece(v, c)], zr.at[owner], oner.at[5], device(v, y, z, c))

    for h in range(2):
        products(h, 0)
    for i in (1, 3, 2):
        for h in range(2):
            for j in (0, 1, 3, 2)[h:]:
                arrive(h, i, j)
            if i != 2:
                cross(h, i)
            products(h, i)

    total = gpart[0]
    for i in range(1, 2 * NX):
        total += gpart[i]
    gsum[...] = total
    go("gram", gsum, gin, oner.at[4], sibling)

    for h in range(2):
        cross(h, 2)
    across = device(x, y, turn(z, ZLO, NZ), core)

    def add_pieces():
        landed(span(zr, OWNERS - 1), oner.at[5])
        total = zsum[piece(x, core), :]
        for v, c in others:
            total += zr[v * 2 + c].astype(F32)
        zown[...] = total.astype(BF16)
        go("across", zown, zpair, oner.at[6], across)

    def add_across():
        landed(zpair, oner.at[6])
        here = piece(x, core)
        zall[here, :] = (zown[...].astype(F32) + zpair[...].astype(F32)).astype(BF16)
        for v, c in others:
            go("back", zall.at[here], zall.at[here], oner.at[7], device(v, y, z, c))

    add_pieces()
    sent("z", span(r3, NZ - 1))
    sent("merged", span(rx, NX - 1))
    sent("tiles", span(r3, NZ - 1))
    sent("gather", span(left, 6 * SUB))
    sent("lines", span(left, 24 * SUB))
    landed(gin, oner.at[4])
    inverse = inverse_factor(gsum[...] + gin[...], ({}, {0: add_across}))
    landed(span(zall, (OWNERS - 1) * PIECE), oner.at[7])
    w1 = inverse.astype(BF16)
    w2 = (inverse - w1.astype(F32)).astype(BF16)

    def apply(matrix, dim):
        dims = (((dim,), (0,)), ((), ()))
        return sum(lax.dot_general(w, matrix, dims, preferred_element_type=F32) for w in (w1, w2))

    factor = (apply(zall[...], 1) / PODS).astype(BF16)
    new_factor[...] = factor.T
    mix = apply(factor, 0)
    head = mix.astype(BF16)
    high[...] = head
    low[...] = (mix - head.astype(F32)).astype(BF16)

    landed(span(left, MINE), oner.at[3])
    load_momentum.wait()
    sent("cross", span(left, MINE))
    sent("gram", gsum)
    sent("right", span(zr, OWNERS - 1))
    sent("across", zown)
    sent("back", span(zr, OWNERS - 1))


def gather(delta, error, momentum, q):
    vmem, hbm = (pl.BlockSpec(memory_space=s) for s in (pltpu.VMEM, pltpu.HBM))
    dma = pltpu.SemaphoreType.DMA
    wide, square = (ROWS, RANK), (RANK, RANK)
    return pl.pallas_call(
        exchange,
        out_shape=(
            jax.ShapeDtypeStruct(wide, BF16),
            jax.ShapeDtypeStruct(wide, BF16),
            jax.ShapeDtypeStruct(wide, BF16),
            jax.ShapeDtypeStruct(square, BF16),
            jax.ShapeDtypeStruct(square, BF16),
            jax.ShapeDtypeStruct(square, BF16),
        ),
        in_specs=[hbm] * 4,
        out_specs=(vmem,) * 6,
        scratch_shapes=[
            pltpu.VMEM(square, BF16),
            pltpu.VMEM(wide, BF16),
            pltpu.VMEM(wide, BF16),
            pltpu.VMEM((MINE, RANK), BF16),
            pltpu.VMEM((MINE, RANK), BF16),
            pltpu.VMEM((NY, NX, SUB, RANK), BF16),
            pltpu.VMEM((NX, NY, SUB, RANK), BF16),
            pltpu.VMEM((2, LINE, RANK), BF16),
            pltpu.VMEM((2, NX, LINE, RANK), BF16),
            pltpu.VMEM((2, LINE, RANK), F32),
            pltpu.VMEM((2, LINE, RANK), BF16),
            pltpu.VMEM((2, NY, SUB, RANK), BF16),
            pltpu.VMEM((2, 2, SUB, HALF), BF16),
            pltpu.VMEM((NZ, 2, TILE, HALF), BF16),
            pltpu.VMEM((2, 2, SUB, HALF), F32),
            pltpu.VMEM((NZ, 2, TILE, HALF), BF16),
            pltpu.VMEM((2 * NX,) + square, F32),
            pltpu.VMEM(square, F32),
            pltpu.VMEM(square, F32),
            pltpu.VMEM(square, F32),
            pltpu.VMEM(square, BF16),
            pltpu.VMEM((OWNERS, PIECE, RANK), BF16),
            pltpu.VMEM((PIECE, RANK), BF16),
            pltpu.VMEM((PIECE, RANK), BF16),
            pltpu.VMEM(square, BF16),
            dma((10,)), dma((13,)), dma((NX,)), dma((2,)), dma((2,)), dma((8,)), dma((2, NY)), dma((2, NX, NY)),
        ],
        compiler_params=pltpu.CompilerParams(collective_id=0, has_side_effects=True, vmem_limit_bytes=32 << 20),
        cost_estimate=pl.CostEstimate(flops=6 * ROWS * RANK * RANK, bytes_accessed=5 * ROWS * RANK * 2, transcendentals=0),
        name="gather_left",
    )(*(pltpu.with_memory_space_constraint(a, pltpu.HBM) for a in (delta, error, momentum, q)))


def finish(left, merged, momentum, high, low, factor, new_error, new_momentum, outer_step, new_factor, e, m, s, sem):
    size, count = ROWS // 8, 8
    copies = [pltpu.make_async_copy(factor, new_factor, sem.at[count, 0])]
    copies[0].start()
    for i in range(count):
        at = pl.ds(i * size, size)
        block = left[at, :]
        approx = jnp.dot(block, high[...], preferred_element_type=F32) + jnp.dot(
            block, low[...], preferred_element_type=F32
        )
        e[at, :] = (merged[at, :].astype(F32) - approx).astype(BF16)
        moment = 0.9 * momentum[at, :].astype(F32) + approx
        m[at, :] = moment.astype(BF16)
        s[at, :] = (0.7 * (approx + 0.9 * moment)).astype(BF16)
        for k, (src, dst) in enumerate(((e, new_error.at[0, at]), (m, new_momentum.at[at]), (s, outer_step.at[at]))):
            copies.append(pltpu.make_async_copy(src.at[at], dst, sem.at[i, k]))
            copies[-1].start()
    for copy in copies:
        copy.wait()


def outputs(left, merged, momentum, high, low, factor):
    any_, vmem = pl.BlockSpec(memory_space=pl.ANY), pl.BlockSpec(memory_space=pltpu.VMEM)
    wide = (ROWS, RANK)
    return pl.pallas_call(
        finish,
        out_shape=(
            jax.ShapeDtypeStruct((1,) + wide, BF16),
            jax.ShapeDtypeStruct(wide, BF16),
            jax.ShapeDtypeStruct(wide, BF16),
            jax.ShapeDtypeStruct((RANK, RANK), BF16),
        ),
        in_specs=[vmem] * 6,
        out_specs=(any_,) * 4,
        scratch_shapes=[pltpu.VMEM(wide, BF16)] * 3 + [pltpu.SemaphoreType.DMA((9, 3))],
        compiler_params=pltpu.CompilerParams(vmem_limit_bytes=24 << 20),
        cost_estimate=pl.CostEstimate(flops=4 * ROWS * RANK * RANK, bytes_accessed=6 * ROWS * RANK * 2, transcendentals=0),
        name="outputs",
    )(left, merged, momentum, high, low, factor)


def body(delta, error, momentum, q_init):
    left, merged, held, high, low, factor = gather(delta, error, momentum, q_init)
    return outputs(left, merged, held, high, low, factor)


def solution(mesh):
    placed = (P("outer", None, "tp"), P("outer", None, "tp"), P(None, "tp"), P("tp", None))
    return jax.shard_map(
        body,
        mesh=mesh,
        in_specs=placed,
        out_specs=(P("outer", None, "tp"), P(None, "tp"), P(None, "tp"), P("tp", None)),
        check_vma=False,
    )
```
